32 devices in a mesh: dp: 8 (over z, y), tensor: 4 (over x, core).
Axes of the slice: x: 2, y: 2, z: 4, core: 2. Of those that a mesh axis runs over, the one named last changes fastest.
Arguments:
- tokens: bfloat16 [8192, 2048], P(('dp', 'tensor')), may hold values from -6 to 6
- segment_ids: int32 [8, 1024], P('dp'), may hold values from 0 to 34, as said below
- mixer_in: bfloat16 [2048, 4, 2048], P('dp', None, 'tensor'), may hold values from -0.125 to 0.125
- mixer_out: bfloat16 [2048, 2048], P('tensor', 'dp'), may hold values from -0.25 to 0.25
- gate_up: bfloat16 [2048, 2, 5632], P('dp', None, 'tensor'), may hold values from -0.125 to 0.125
- down: bfloat16 [5632, 2048], P('tensor', 'dp'), may hold values from -0.15625 to 0.15625
- norm_gain: bfloat16 [2048], P('dp'), may hold values from 0.25 to 1.75
- group_gain: bfloat16 [128], P('dp'), may hold values from 0.25 to 1.75
- ffn_gain: bfloat16 [2048], P('dp'), may hold values from 0.25 to 1.75
- cotangent: bfloat16 [8192, 2048], P(('dp', 'tensor')), may hold values from -6 to 6
Outputs:
- output: bfloat16 [8192, 2048], P(('dp', 'tensor'))
- d_tokens: bfloat16 [8192, 2048], P(('dp', 'tensor'))
- d_mixer_in: float32 [2048, 4, 2048], P('dp', None, 'tensor')
- d_mixer_out: float32 [2048, 2048], P('tensor', 'dp')
- d_gate_up: float32 [2048, 2, 5632], P('dp', None, 'tensor')
- d_down: float32 [5632, 2048], P('tensor', 'dp')
- d_norm_gain: float32 [2048], P('dp')
- d_group_gain: float32 [128], P('dp')
- d_ffn_gain: float32 [2048], P('dp')
The draws below stay inside these ranges and needn't reach their ends.
Inputs may be any that keep to these rules, and one draw needn't show every extreme that they name: `segment_ids`: each row counts documents from 0 upward and never falls, and holds exactly 35 documents; one of them begins before position 128 and ends at position 896 or later, and the rest are short.
All inputs are finite; a program needn't handle non-finite values.
Results may differ from the reference program's by a relative error of at most 0.023.
The reference program's roundings to bfloat16 on the way count: a program that leaves them out, or rounds other values in their place, can miss the bound.
Values may be sent and summed in bfloat16 or wider, within the bound.
No kernel may reach another device: no remote copies, remote signals or barrier semaphores. Data moves between devices by JAX's collectives and lax.ppermute only.
A program may use at most 256 MiB of HBM per device.

```python
import jax
import jax.numpy as jnp
from jax import lax

D = 2048
HD = 128
FF = 5632
TOK_DEV = 256
SPAN = 64
SEQ = 1024
TOKENS = 8192
N_DP = 8


def draw_segment_ids(key, part):
    key = jax.random.fold_in(key, 11)
    first_key, second_key, third_key = jax.random.split(key, 3)
    margin = max(TOK_DEV // 2, 2)
    shorts = max(TOK_DEV // 8, 1)
    first = jax.random.randint(first_key, (N_DP, 1), shorts + 1, margin)
    ending = SEQ - jax.random.randint(second_key, (N_DP, 1), 1, margin)
    position = jnp.arange(SEQ, dtype=jnp.int32)[None, :]
    outside = jnp.logical_or(position < first, position > ending)
    candidate = jnp.logical_and(outside, position > 0)
    row_keys = jax.random.split(third_key, N_DP)
    orders = jax.vmap(lambda row_key: jax.random.permutation(row_key, SEQ))(row_keys).astype(jnp.int32)
    scores = jnp.where(candidate, orders, -1)
    _, chosen = lax.top_k(scores, shorts)
    picked = jnp.any(position[:, :, None] == chosen[:, None, :].astype(jnp.int32), axis=2)
    starts = jnp.logical_or(picked, jnp.logical_or(position == first, position == ending))
    return jnp.cumsum(starts.astype(jnp.int32), axis=1).astype(jnp.int32)


def shard_levels(stream_key, shape, cuts, low, high):
    def one(dim, parts):
        draws = jax.random.uniform(jax.random.fold_in(jax.random.fold_in(stream_key, 6), dim), (parts,), jnp.float32, low / len(cuts), high / len(cuts))
        return jnp.repeat(jnp.exp(draws), shape[dim] // parts).reshape((-1,) + (1,) * (len(shape) - dim - 1))

    loudness = one(*cuts[0])
    for cut in cuts[1:]:
        loudness = loudness * one(*cut)
    return loudness


def scatter_about(rng, shape, scale, most, cuts=(), kind=jnp.bfloat16):
    entries = scale * jax.random.normal(rng, shape, jnp.float32)
    if cuts:
        entries = entries * shard_levels(rng, shape, cuts, -0.22, 0.18)
    return jnp.clip(entries, -most, most).astype(kind)


def setup_inputs(seed: int = 0) -> dict:
    streams_of = jax.random.split(jax.random.key(seed), 11)
    return {
        "tokens": scatter_about(streams_of[0], (TOKENS, D), 1.0, 6.0, ((0, 32),)),
        "segment_ids": draw_segment_ids(jax.random.fold_in(streams_of[10], 71), 0),
        "mixer_in": scatter_about(streams_of[2], (D, 4, D), D ** -0.5, 0.125, ((0, 8), (2, 4))),
        "mixer_out": scatter_about(streams_of[3], (D, D), (D // 4) ** -0.5, 0.25, ((0, 4), (1, 8))),
        "gate_up": scatter_about(streams_of[4], (D, 2, FF), D ** -0.5, 0.125, ((0, 8), (2, 4))),
        "down": scatter_about(streams_of[5], (FF, D), (FF // 4) ** -0.5, 0.15625, ((0, 4), (1, 8))),
        "norm_gain": jnp.clip(1.0 + 0.15 * jax.random.normal(streams_of[6], (D,), jnp.float32), 0.25, 1.75).astype(jnp.bfloat16),
        "group_gain": jnp.clip(1.0 + 0.15 * jax.random.normal(streams_of[7], (HD,), jnp.float32), 0.25, 1.75).astype(jnp.bfloat16),
        "ffn_gain": jnp.clip(1.0 + 0.15 * jax.random.normal(streams_of[8], (D,), jnp.float32), 0.25, 1.75).astype(jnp.bfloat16),
        "cotangent": scatter_about(streams_of[9], (TOKENS, D), 1.0, 6.0, ((0, 32),)),
    }


EPSILON = 1e-06
GROUP_EPSILON = 0.01
FORGET_FLOOR = 0.8
HIGHEST = lax.Precision.HIGHEST

@jax.custom_vjp
def low(v):
    return lax.optimization_barrier(v.astype(jnp.bfloat16)).astype(jnp.float32)

@jax.custom_vjp
def low_back(v):
    return v

def low_keep(v):
    return (low(v), None)

def low_pass(kept, grad):
    return (grad,)

def back_keep(v):
    return (v, None)

def back_low(kept, grad):
    return (low(grad),)
low.defvjp(low_keep, low_pass)
low_back.defvjp(back_keep, back_low)

def rms_norm(values, gain, offset=EPSILON):
    return values * lax.rsqrt(lax.optimization_barrier(jnp.mean(values * values, axis=-1, keepdims=True)) + offset) * gain

def mixer_core(query, forget_raw, inputs, out_gate, group_weight, doc_ids):
    length = query.shape[0]
    width = query.shape[1]
    heads = width // HD
    blocks = length // SPAN
    forget = FORGET_FLOOR + (1.0 - FORGET_FLOOR) * jax.nn.sigmoid(forget_raw)
    decay_logs = jnp.log(forget)
    key_rows = 1.0 - forget

    def split_blocks(array):
        return array.reshape(blocks, SPAN, heads, HD)
    cumulative = jnp.cumsum(split_blocks(decay_logs), axis=1)
    doc_blocks = doc_ids.reshape(blocks, SPAN)
    causal = jnp.arange(SPAN)[:, None] >= jnp.arange(SPAN)[None, :]

    def block_step(carry, item):
        memory, last_doc = carry
        query_block, key_block, input_block, cum_block, doc_block = item
        query_decay = query_block * jnp.exp(cum_block)
        key_decay = key_block * jnp.exp(-cum_block)
        scores = jnp.einsum('thc,shc->hts', query_decay, key_decay, precision=HIGHEST)
        same_doc = jnp.logical_and(causal, doc_block[:, None] == doc_block[None, :])
        scores = jnp.where(same_doc[None], scores, 0.0)
        within = jnp.einsum('hts,she->the', scores, input_block, precision=HIGHEST)
        continued = (doc_block == last_doc).astype(jnp.float32)
        earlier = jnp.einsum('thc,hce->the', query_decay, memory, precision=HIGHEST) * continued[:, None, None]
        total_decay = cum_block[-1]
        end_doc = doc_block[-1]
        tail_rows = (doc_block == end_doc).astype(jnp.float32)
        key_tail = key_block * jnp.exp(total_decay[None] - cum_block) * tail_rows[:, None, None]
        kept_memory = memory * jnp.exp(total_decay)[:, :, None] * (end_doc == last_doc).astype(jnp.float32)
        memory = kept_memory + jnp.einsum('shc,she->hce', key_tail, input_block, precision=HIGHEST)
        return ((memory, end_doc), within + earlier)
    initial = (jnp.zeros((heads, HD, HD), jnp.float32), jnp.array(-1, jnp.int32))
    _, mixed = lax.scan(jax.checkpoint(block_step), initial, (split_blocks(query), split_blocks(key_rows), split_blocks(inputs), cumulative, doc_blocks))
    mixed = mixed.reshape(length, heads, HD)
    normed = rms_norm(mixed, group_weight, GROUP_EPSILON)
    gate_heads = out_gate.reshape(length, heads, HD)
    return (normed * jax.nn.silu(gate_heads)).reshape(length, width)

def layer(rows, doc_ids, w_in, w_out, w_gu, w_down, gain_in, gain_group, gain_ffn):
    normed_in = low(rms_norm(rows, gain_in))
    projected = jnp.einsum('td,dkc->tkc', normed_in, w_in, precision=HIGHEST)
    projected = low_back(low(projected))
    mixed = low(mixer_core(projected[:, 0], projected[:, 1], projected[:, 2], projected[:, 3], gain_group, doc_ids))
    attention = low_back(jnp.dot(mixed, w_out, precision=HIGHEST))
    resid = rows + attention
    normed_ffn = low(rms_norm(resid, gain_ffn))
    gate_up_vals = low_back(jnp.einsum('td,dkc->tkc', normed_ffn, w_gu, precision=HIGHEST))
    hidden = low(jax.nn.silu(gate_up_vals[:, 0]) * gate_up_vals[:, 1])
    ffn_out = low_back(jnp.dot(hidden, w_down, precision=HIGHEST))
    return resid + ffn_out

def reference(tokens, segment_ids, mixer_in, mixer_out, gate_up, down, norm_gain, group_gain, ffn_gain, cotangent):

    def forward(rows, w_in, w_out, w_gu, w_down, gain_in, gain_group, gain_ffn):

        def group_step(carry, item):
            group_rows, doc_ids = item
            return (carry, layer(group_rows, doc_ids, w_in, w_out, w_gu, w_down, gain_in, gain_group, gain_ffn))
        _, result = lax.scan(jax.checkpoint(group_step), None, (rows.reshape(N_DP, SEQ, D), segment_ids))
        return result.reshape(TOKENS, D)
    floats = [array.astype(jnp.float32) for array in (tokens, mixer_in, mixer_out, gate_up, down, norm_gain, group_gain, ffn_gain)]
    output, backward = jax.vjp(forward, *floats)
    grads = backward(cotangent.astype(jnp.float32))
    return (output.astype(jnp.bfloat16), grads[0].astype(jnp.bfloat16), grads[1], grads[2], grads[3], grads[4], grads[5], grads[6], grads[7])
```

```python
import functools
import jax
import jax.numpy as jnp
from jax import lax
from jax.experimental import pallas as pl
from jax.experimental.pallas import tpu as pltpu
from jax.sharding import PartitionSpec as P

HD = 128
CHUNK = 128
GROUP_EPSILON = 0.01
F32 = jnp.float32
BF16 = jnp.bfloat16
NN = (((1,), (0,)), ((), ()))
NT = (((1,), (1,)), ((), ()))
TN = (((0,), (0,)), ((), ()))


def mm(a, b, dims):
    return lax.dot_general(a, b, dims, preferred_element_type=F32)


def halves(x):
    high = x.astype(BF16)
    return high, (x - high.astype(F32)).astype(BF16)


def tri_sum(tri, x):
    high, rest = halves(x)
    return mm(tri, high, NN) + mm(tri, rest, NN)


def decays(a_raw, lower):
    sig = jax.nn.sigmoid(a_raw)
    forget = 0.8 + 0.2 * sig
    key = 1.0 - forget
    cum = tri_sum(lower, jnp.log(forget))
    return sig, forget, key, cum


def masks(seg, doc_col, doc_row, block):
    rows = lax.broadcasted_iota(jnp.int32, (CHUNK, CHUNK), 0)
    cols = lax.broadcasted_iota(jnp.int32, (CHUNK, CHUNK), 1)
    causal = rows >= cols
    same = jnp.logical_and(causal, doc_col == doc_row)
    start = block * CHUNK
    end_doc = seg[start + CHUNK - 1]
    last_doc = jnp.where(block > 0, seg[jnp.maximum(start - 1, 0)], -1)
    cont = (doc_col == last_doc).astype(F32)
    tail = (doc_col == end_doc).astype(F32)
    keep = jnp.where(end_doc == last_doc, 1.0, 0.0).astype(F32)
    return causal, same, cont, tail, keep


def forward_kernel(seg, q_ref, a_ref, v_ref, z_ref, col_ref, row_ref, gain_ref,
                   y_ref, o_ref, s_ref, state):
    block = pl.program_id(0)

    @pl.when(block == 0)
    def _():
        state[...] = jnp.zeros_like(state)

    width = q_ref.shape[1]
    causal, same, cont, tail, keep = masks(seg, col_ref[...], row_ref[...], block)
    lower = jnp.where(causal, 1.0, 0.0).astype(BF16)
    _, _, key, cum = decays(a_ref[...].astype(F32), lower)
    total = cum[CHUNK - 1 : CHUNK, :]
    qd, qd_rest = halves(q_ref[...].astype(F32) * jnp.exp(cum))
    kd, kd_rest = halves(key * jnp.exp(-cum))
    kt, kt_rest = halves(key * jnp.exp(total - cum) * tail)
    fade = jnp.exp(total) * keep
    gain = gain_ref[...]
    s_ref[0] = state[...]
    for head in range(width // HD):
        at = slice(head * HD, (head + 1) * HD)
        v = v_ref[:, at]
        st = state[:, at]
        st_high, st_rest = halves(st)
        qh, ql = qd[:, at], qd_rest[:, at]
        scores = mm(qh, kd[:, at], NT) + (mm(qh, kd_rest[:, at], NT) + mm(ql, kd[:, at], NT))
        scores = jnp.where(same, scores, 0.0).astype(BF16)
        earlier = mm(qh, st_high, NT) + (mm(qh, st_rest, NT) + mm(ql, st_high, NT))
        o = mm(scores, v, NN) + cont * earlier
        state[:, at] = st * fade[:, at] + (mm(v, kt[:, at], TN) + mm(v, kt_rest[:, at], TN))
        o_ref[:, at] = o
        z = z_ref[:, at].astype(F32)
        r = lax.rsqrt(jnp.mean(o * o, axis=-1, keepdims=True) + GROUP_EPSILON)
        y_ref[:, at] = (o * r * gain * (z * jax.nn.sigmoid(z))).astype(BF16)


def backward_kernel(seg, q_ref, a_ref, v_ref, z_ref, col_ref, row_ref, gain_ref, o_ref, s_ref, dy_ref,
                    d_ref, dgain_ref, dstate):
    step = pl.program_id(0)
    block = pl.num_programs(0) - 1 - step

    @pl.when(step == 0)
    def _():
        dstate[...] = jnp.zeros_like(dstate)
        dgain_ref[...] = jnp.zeros_like(dgain_ref)

    width = q_ref.shape[1]
    causal, same, cont, tail, keep = masks(seg, col_ref[...], row_ref[...], block)
    lower = jnp.where(causal, 1.0, 0.0).astype(BF16)
    sig, forget, key, cum = decays(a_ref[...].astype(F32), lower)
    total = cum[CHUNK - 1 : CHUNK, :]
    up = jnp.exp(cum)
    down = jnp.exp(-cum)
    late = jnp.exp(total - cum) * tail
    qd = (q_ref[...].astype(F32) * up).astype(BF16)
    kd = (key * down).astype(BF16)
    kt = (key * late).astype(BF16)
    fade = jnp.exp(total) * keep
    gain = gain_ref[...]
    gain_sum = jnp.zeros((1, HD), F32)
    dcums = []
    dkeys = []
    for head in range(width // HD):
        at = slice(head * HD, (head + 1) * HD)
        v = v_ref[:, at]
        o = o_ref[:, at]
        z = z_ref[:, at].astype(F32)
        dy = dy_ref[:, at]
        r = lax.rsqrt(jnp.mean(o * o, axis=-1, keepdims=True) + GROUP_EPSILON)
        n = o * r
        sz = jax.nn.sigmoid(z)
        dng = dy * (z * sz)
        gain_sum += jnp.sum(dng * n, axis=0, keepdims=True)
        dn = dng * gain
        do = (r * (dn - n * jnp.mean(dn * n, axis=-1, keepdims=True))).astype(BF16)
        d_ref[:, 3 * width + head * HD : 3 * width + (head + 1) * HD] = (
            dy * n * gain * (sz * (1.0 + z * (1.0 - sz)))
        ).astype(BF16)
        qh, kh, th = qd[:, at], kd[:, at], kt[:, at]
        scores = jnp.where(same, mm(qh, kh, NT), 0.0).astype(BF16)
        dscores = jnp.where(same, mm(do, v, NT), 0.0).astype(BF16)
        st = s_ref[0, :, at]
        dst = dstate[:, at]
        dst_low = dst.astype(BF16)
        dv = mm(scores, do, TN) + mm(th, dst_low, NT)
        dqd = mm(dscores, kh, NN) + cont * mm(do, st.astype(BF16), NN)
        dkd = mm(dscores, qh, TN)
        dkt = mm(v, dst_low, NN)
        carried = dkt * th.astype(F32)
        dtotal = jnp.sum(carried, axis=0, keepdims=True) + fade[:, at] * jnp.sum(
            dst * st, axis=0, keepdims=True
        )
        dstate[:, at] = dst * fade[:, at] + mm((do.astype(F32) * cont).astype(BF16), qh, TN)
        d_ref[:, head * HD : (head + 1) * HD] = (dqd * up[:, at]).astype(BF16)
        d_ref[:, 2 * width + head * HD : 2 * width + (head + 1) * HD] = dv.astype(BF16)
        dkeys.append(dkd * down[:, at] + dkt * late[:, at])
        dcum = dqd * qh.astype(F32) - dkd * kh.astype(F32) - carried
        high, rest = halves(dcum)
        dlog = mm(lower, high, TN) + mm(lower, rest, TN) + dtotal
        slope = 0.2 * sig[:, at] * (1.0 - sig[:, at])
        d_ref[:, width + head * HD : width + (head + 1) * HD] = (
            (dlog / forget[:, at] - dkeys[-1]) * slope
        ).astype(BF16)
    dgain_ref[...] += gain_sum


def rec_forward(proj, seg, gain):
    length, width = proj.shape[0], proj.shape[1] // 4
    blocks = length // CHUNK
    part = lambda k: pl.BlockSpec((CHUNK, width), lambda i, s, k=k: (i, k))
    return pl.pallas_call(
        forward_kernel,
        grid_spec=pltpu.PrefetchScalarGridSpec(
            num_scalar_prefetch=1,
            grid=(blocks,),
            in_specs=[part(0), part(1), part(2), part(3),
                      pl.BlockSpec((CHUNK, 1), lambda i, s: (i, 0)),
                      pl.BlockSpec((1, CHUNK), lambda i, s: (0, i)),
                      pl.BlockSpec((1, HD), lambda i, s: (0, 0))],
            out_specs=[pl.BlockSpec((CHUNK, width), lambda i, s: (i, 0)),
                       pl.BlockSpec((CHUNK, width), lambda i, s: (i, 0)),
                       pl.BlockSpec((1, HD, width), lambda i, s: (i, 0, 0))],
            scratch_shapes=[pltpu.VMEM((HD, width), F32)],
        ),
        out_shape=[jax.ShapeDtypeStruct((length, width), BF16),
                   jax.ShapeDtypeStruct((length, width), F32),
                   jax.ShapeDtypeStruct((blocks, HD, width), F32)],
        cost_estimate=pl.CostEstimate(flops=30_000_000_000, bytes_accessed=10_000_000, transcendentals=0),
        name="mixer_forward",
    )(seg, proj, proj, proj, proj, seg.reshape(length, 1), seg.reshape(1, length), gain.reshape(1, HD))


def rec_backward(proj, seg, gain, o, states, dy):
    length, width = proj.shape[0], proj.shape[1] // 4
    blocks = length // CHUNK
    last = blocks - 1
    part = lambda k: pl.BlockSpec((CHUNK, width), lambda i, s, k=k: (last - i, k))
    return pl.pallas_call(
        backward_kernel,
        grid_spec=pltpu.PrefetchScalarGridSpec(
            num_scalar_prefetch=1,
            grid=(blocks,),
            in_specs=[part(0), part(1), part(2), part(3),
                      pl.BlockSpec((CHUNK, 1), lambda i, s: (last - i, 0)),
                      pl.BlockSpec((1, CHUNK), lambda i, s: (0, last - i)),
                      pl.BlockSpec((1, HD), lambda i, s: (0, 0)),
                      part(0),
                      pl.BlockSpec((1, HD, width), lambda i, s: (last - i, 0, 0)),
                      part(0)],
            out_specs=[pl.BlockSpec((CHUNK, 4 * width), lambda i, s: (last - i, 0)),
                       pl.BlockSpec((1, HD), lambda i, s: (0, 0))],
            scratch_shapes=[pltpu.VMEM((HD, width), F32)],
        ),
        out_shape=[jax.ShapeDtypeStruct((length, 4 * width), BF16),
                   jax.ShapeDtypeStruct((1, HD), F32)],
        cost_estimate=pl.CostEstimate(flops=60_000_000_000, bytes_accessed=14_000_000, transcendentals=0),
        name="mixer_backward",
    )(seg, proj, proj, proj, proj, seg.reshape(length, 1), seg.reshape(1, length), gain.reshape(1, HD), o, states, dy)


EPSILON = 1e-06
SPEC_ROWS = P(("dp", "tensor"), None)


def ring_order(count):
    return list(range(0, count, 2)) + list(range(count - 1 - count % 2, 0, -2))


class Ring:
    def __init__(self, axis, count):
        order = ring_order(count)
        self.axis, self.count = axis, count
        self.order = jnp.array(order, jnp.int32)
        self.ahead = [(order[i], order[(i + 1) % count]) for i in range(count)]
        self.behind = [(b, a) for a, b in self.ahead]
        place = [order.index(i) for i in range(count)]
        self.me = lax.axis_index(axis)
        self.place = jnp.array(place, jnp.int32)[self.me]

    def owner(self, shift):
        return self.order[(self.place + shift + 2 * self.count) % self.count]

    def send_ahead(self, x):
        return lax.ppermute(x, self.axis, self.ahead)

    def send_behind(self, x):
        return lax.ppermute(x, self.axis, self.behind)

    def gather(self, x, dim):
        size = x.shape[dim]
        half = x.shape[0] // 2
        shape = list(x.shape)
        shape[dim] *= self.count

        def put(whole, block, owner, row=0):
            at = [row, 0]
            at[dim] = at[dim] + owner * size
            return lax.dynamic_update_slice(whole, block, at)

        whole = put(jnp.zeros(shape, x.dtype), x, self.me)
        left = right = x
        steps = self.count // 2
        for step in range(1, steps):
            left, right = self.send_ahead(left), self.send_behind(right)
            whole = put(whole, left, self.owner(-step))
            whole = put(whole, right, self.owner(step))
        left, right = self.send_ahead(left[:half]), self.send_behind(right[half:])
        whole = put(whole, left, self.owner(-steps))
        return put(whole, right, self.owner(steps), half)

    def scatter_sum(self, x, dim):
        shape = list(x.shape)
        shape[dim] //= self.count
        size, half = shape[dim], shape[0] // 2
        shape[0] = half

        def part(shift, row):
            at = [row, 0]
            at[dim] = at[dim] + self.owner(shift) * size
            return lax.dynamic_slice(x, at, shape)

        left, right = part(-1, 0), part(1, half)
        for step in range(1, self.count):
            left, right = self.send_ahead(left), self.send_behind(right)
            own_left, own_right = part(-1 - step, 0), part(1 + step, half)
            if step == self.count - 1:
                left, right = left.astype(F32), right.astype(F32)
                own_left, own_right = own_left.astype(F32), own_right.astype(F32)
            left, right = left + own_left, right + own_right
        return jnp.concatenate([left, right], axis=0)


def gather_small(row, axis, count):
    me = lax.axis_index(axis)
    whole = lax.dynamic_update_slice(jnp.zeros((count, row.shape[1]), row.dtype), row, (me, 0))
    for turn in range(1, count):
        got = lax.ppermute(row, axis, [(i, (i + turn) % count) for i in range(count)])
        whole = lax.dynamic_update_slice(whole, got, ((me - turn + count) % count, 0))
    return whole


def scatter_sum_small(rows, axis, count):
    me = lax.axis_index(axis)
    total = lax.dynamic_slice_in_dim(rows, me, 1, 0)
    for turn in range(1, count):
        mine = lax.dynamic_slice_in_dim(rows, (me + turn) % count, 1, 0)
        total = total + lax.ppermute(mine, axis, [(i, (i + turn) % count) for i in range(count)])
    return total


def norm_forward(values, gain):
    r = lax.rsqrt(jnp.mean(values * values, axis=-1, keepdims=True) + EPSILON)
    return (values * r * gain).astype(BF16), r


def norm_backward(values, r, gain, grad):
    n = values * r
    scaled = grad * gain
    back = r * (scaled - n * jnp.mean(scaled * n, axis=-1, keepdims=True))
    return back, jnp.sum(grad * n, axis=0)


def tensor_gather(x):
    return lax.all_gather(x, "tensor", axis=0, tiled=True)


def tensor_scatter_sum(x):
    return lax.psum_scatter(x, "tensor", scatter_dimension=0, tiled=True).astype(F32)


def body(n_dp, n_tensor, tokens, segment_ids, mixer_in, mixer_out, gate_up, down,
         norm_gain, group_gain, ffn_gain, cotangent):
    ring = Ring("dp", n_dp)
    seg = segment_ids[0]
    x = tokens.astype(F32)
    part, small = norm_gain.shape[0], group_gain.shape[0]
    model = part * n_dp
    width = mixer_out.shape[0]
    hidden_width = down.shape[0]

    gains = gather_small(jnp.concatenate([norm_gain, ffn_gain, group_gain]).astype(F32)[None], "dp", n_dp)
    gain_in = gains[:, :part].reshape(1, model)
    gain_ffn = gains[:, part : 2 * part].reshape(1, model)
    gain_group = gains[:, 2 * part :].reshape(1, HD)

    w_in = ring.gather(mixer_in.reshape(part, 4 * width), 0)
    w_out = ring.gather(mixer_out, 1)
    w_gu = ring.gather(gate_up.reshape(part, 2 * hidden_width), 0)
    w_down = ring.gather(down, 1)

    h1_own, r1 = norm_forward(x, gain_in)
    h1 = tensor_gather(h1_own)
    cot = tensor_gather(cotangent)
    proj = mm(h1, w_in, NN).astype(BF16)
    y, o, states = rec_forward(proj, seg, gain_group)
    attn = tensor_scatter_sum(mm(y, w_out, NN).astype(BF16))
    x2 = x + attn
    h2_own, r2 = norm_forward(x2, gain_ffn)
    h2 = tensor_gather(h2_own)
    gu = mm(h2, w_gu, NN)
    gate, up = gu[:, :hidden_width], gu[:, hidden_width:]
    sg = jax.nn.sigmoid(gate)
    swish = gate * sg
    hidden = (swish * up).astype(BF16)
    d_down = ring.scatter_sum(mm(hidden, cot, TN).astype(BF16), 1)
    dh = mm(cot, w_down, NT)
    dgate = (dh * up * sg * (1.0 + gate * (1.0 - sg))).astype(BF16)
    dup = (dh * swish).astype(BF16)
    dgu = jnp.concatenate([dgate, dup], axis=1)
    d_gu = ring.scatter_sum(mm(h2, dgu, TN).astype(BF16), 0)
    dh2 = tensor_scatter_sum(mm(dgu, w_gu, NT).astype(BF16))
    back2, d_gain_ffn = norm_backward(x2, r2, gain_ffn, dh2)
    dx2 = cotangent.astype(F32) + back2
    dattn = tensor_gather(dx2.astype(BF16))
    d_out = ring.scatter_sum(mm(y, dattn, TN).astype(BF16), 1)
    dy = mm(dattn, w_out, NT)
    dproj, d_group = rec_backward(proj, seg, gain_group, o, states, dy)
    d_in = ring.scatter_sum(mm(h1, dproj, TN).astype(BF16), 0)
    dh1 = tensor_scatter_sum(mm(dproj, w_in, NT).astype(BF16))
    back1, d_gain_in = norm_backward(x, r1, gain_in, dh1)
    d_tokens = (dx2 + back1).astype(BF16)
    output = (x2 + tensor_scatter_sum(mm(hidden, w_down, NN).astype(BF16))).astype(BF16)

    d_gains = jnp.concatenate(
        [d_gain_in.reshape(n_dp, part), d_gain_ffn.reshape(n_dp, part), d_group.reshape(n_dp, small)], axis=1
    )
    d_gains = scatter_sum_small(lax.psum(d_gains, "tensor"), "dp", n_dp)[0]
    return (
        output,
        d_tokens,
        d_in.reshape(part, 4, width),
        d_out,
        d_gu.reshape(part, 2, hidden_width),
        d_down,
        d_gains[:part],
        d_gains[2 * part :],
        d_gains[part : 2 * part],
    )


def solution(mesh):
    split = P("dp", None, "tensor")
    cross = P("tensor", "dp")
    return jax.shard_map(
        functools.partial(body, mesh.shape["dp"], mesh.shape["tensor"]),
        mesh=mesh,
        in_specs=(SPEC_ROWS, P("dp", None), split, cross, split, cross, P("dp"), P("dp"), P("dp"), SPEC_ROWS),
        out_specs=(SPEC_ROWS, SPEC_ROWS, split, cross, split, cross, P("dp"), P("dp"), P("dp")),
        check_vma=False,
    )
```

```python
import functools
import jax
import jax.numpy as jnp
from jax import lax
from jax.experimental import pallas as pl
from jax.experimental.pallas import tpu as pltpu
from jax.sharding import PartitionSpec as P

HD = 128
CHUNK = 128
GROUP_EPSILON = 0.01
F32 = jnp.float32
BF16 = jnp.bfloat16
NN = (((1,), (0,)), ((), ()))
NT = (((1,), (1,)), ((), ()))
TN = (((0,), (0,)), ((), ()))


def mm(a, b, dims):
    return lax.dot_general(a, b, dims, preferred_element_type=F32)


def halves(x):
    high = x.astype(BF16)
    return high, (x - high.astype(F32)).astype(BF16)


def tri_sum(tri, x):
    high, rest = halves(x)
    return mm(tri, high, NN) + mm(tri, rest, NN)


def decays(a_raw, lower):
    sig = jax.nn.sigmoid(a_raw)
    forget = 0.8 + 0.2 * sig
    key = 1.0 - forget
    cum = tri_sum(lower, jnp.log(forget))
    return sig, forget, key, cum


def masks(seg, doc_col, doc_row, block):
    rows = lax.broadcasted_iota(jnp.int32, (CHUNK, CHUNK), 0)
    cols = lax.broadcasted_iota(jnp.int32, (CHUNK, CHUNK), 1)
    causal = rows >= cols
    same = jnp.logical_and(causal, doc_col == doc_row)
    start = block * CHUNK
    end_doc = seg[start + CHUNK - 1]
    last_doc = jnp.where(block > 0, seg[jnp.maximum(start - 1, 0)], -1)
    cont = (doc_col == last_doc).astype(F32)
    tail = (doc_col == end_doc).astype(F32)
    keep = jnp.where(end_doc == last_doc, 1.0, 0.0).astype(F32)
    return causal, same, cont, tail, keep


def forward_kernel(seg, q_ref, a_ref, v_ref, z_ref, col_ref, row_ref, gain_ref,
                   y_ref, o_ref, s_ref, state):
    block = pl.program_id(0)

    @pl.when(block == 0)
    def _():
        state[...] = jnp.zeros_like(state)

    width = q_ref.shape[1]
    causal, same, cont, tail, keep = masks(seg, col_ref[...], row_ref[...], block)
    lower = jnp.where(causal, 1.0, 0.0).astype(BF16)
    _, _, key, cum = decays(a_ref[...].astype(F32), lower)
    total = cum[CHUNK - 1 : CHUNK, :]
    qd, qd_rest = halves(q_ref[...].astype(F32) * jnp.exp(cum))
    kd, kd_rest = halves(key * jnp.exp(-cum))
    kt, kt_rest = halves(key * jnp.exp(total - cum) * tail)
    fade = jnp.exp(total) * keep
    gain = gain_ref[...]
    s_ref[0] = state[...]
    for head in range(width // HD):
        at = slice(head * HD, (head + 1) * HD)
        v = v_ref[:, at]
        st = state[:, at]
        st_high, st_rest = halves(st)
        qh, ql = qd[:, at], qd_rest[:, at]
        scores = mm(qh, kd[:, at], NT) + (mm(qh, kd_rest[:, at], NT) + mm(ql, kd[:, at], NT))
        scores = jnp.where(same, scores, 0.0).astype(BF16)
        earlier = mm(qh, st_high, NT) + (mm(qh, st_rest, NT) + mm(ql, st_high, NT))
        o = mm(scores, v, NN) + cont * earlier
        state[:, at] = st * fade[:, at] + (mm(v, kt[:, at], TN) + mm(v, kt_rest[:, at], TN))
        o_ref[:, at] = o
        z = z_ref[:, at].astype(F32)
        r = lax.rsqrt(jnp.mean(o * o, axis=-1, keepdims=True) + GROUP_EPSILON)
        y_ref[:, at] = (o * r * gain * (z * jax.nn.sigmoid(z))).astype(BF16)


def backward_kernel(seg, q_ref, a_ref, v_ref, z_ref, col_ref, row_ref, gain_ref, o_ref, s_ref, dy_ref,
                    d_ref, dgain_ref, dstate):
    step = pl.program_id(0)
    block = pl.num_programs(0) - 1 - step

    @pl.when(step == 0)
    def _():
        dstate[...] = jnp.zeros_like(dstate)
        dgain_ref[...] = jnp.zeros_like(dgain_ref)

    width = q_ref.shape[1]
    causal, same, cont, tail, keep = masks(seg, col_ref[...], row_ref[...], block)
    lower = jnp.where(causal, 1.0, 0.0).astype(BF16)
    sig, forget, key, cum = decays(a_ref[...].astype(F32), lower)
    total = cum[CHUNK - 1 : CHUNK, :]
    up = jnp.exp(cum)
    down = jnp.exp(-cum)
    late = jnp.exp(total - cum) * tail
    qd = (q_ref[...].astype(F32) * up).astype(BF16)
    kd = (key * down).astype(BF16)
    kt = (key * late).astype(BF16)
    fade = jnp.exp(total) * keep
    gain = gain_ref[...]
    gain_sum = jnp.zeros((1, HD), F32)
    dcums = []
    dkeys = []
    for head in range(width // HD):
        at = slice(head * HD, (head + 1) * HD)
        v = v_ref[:, at]
        o = o_ref[:, at]
        z = z_ref[:, at].astype(F32)
        dy = dy_ref[:, at]
        r = lax.rsqrt(jnp.mean(o * o, axis=-1, keepdims=True) + GROUP_EPSILON)
        n = o * r
        sz = jax.nn.sigmoid(z)
        dng = dy * (z * sz)
        gain_sum += jnp.sum(dng * n, axis=0, keepdims=True)
        dn = dng * gain
        do = (r * (dn - n * jnp.mean(dn * n, axis=-1, keepdims=True))).astype(BF16)
        d_ref[:, 3 * width + head * HD : 3 * width + (head + 1) * HD] = (
            dy * n * gain * (sz * (1.0 + z * (1.0 - sz)))
        ).astype(BF16)
        qh, kh, th = qd[:, at], kd[:, at], kt[:, at]
        scores = jnp.where(same, mm(qh, kh, NT), 0.0).astype(BF16)
        dscores = jnp.where(same, mm(do, v, NT), 0.0).astype(BF16)
        st = s_ref[0, :, at]
        dst = dstate[:, at]
        dst_low = dst.astype(BF16)
        dv = mm(scores, do, TN) + mm(th, dst_low, NT)
        dqd = mm(dscores, kh, NN) + cont * mm(do, st.astype(BF16), NN)
        dkd = mm(dscores, qh, TN)
        dkt = mm(v, dst_low, NN)
        carried = dkt * th.astype(F32)
        dtotal = jnp.sum(carried, axis=0, keepdims=True) + fade[:, at] * jnp.sum(
            dst * st, axis=0, keepdims=True
        )
        dstate[:, at] = dst * fade[:, at] + mm((do.astype(F32) * cont).astype(BF16), qh, TN)
        d_ref[:, head * HD : (head + 1) * HD] = (dqd * up[:, at]).astype(BF16)
        d_ref[:, 2 * width + head * HD : 2 * width + (head + 1) * HD] = dv.astype(BF16)
        dkeys.append(dkd * down[:, at] + dkt * late[:, at])
        dcum = dqd * qh.astype(F32) - dkd * kh.astype(F32) - carried
        high, rest = halves(dcum)
        dlog = mm(lower, high, TN) + mm(lower, rest, TN) + dtotal
        slope = 0.2 * sig[:, at] * (1.0 - sig[:, at])
        d_ref[:, width + head * HD : width + (head + 1) * HD] = (
            (dlog / forget[:, at] - dkeys[-1]) * slope
        ).astype(BF16)
    dgain_ref[...] += gain_sum


def rec_forward(proj, seg, gain):
    length, width = proj.shape[0], proj.shape[1] // 4
    blocks = length // CHUNK
    part = lambda k: pl.BlockSpec((CHUNK, width), lambda i, s, k=k: (i, k))
    return pl.pallas_call(
        forward_kernel,
        grid_spec=pltpu.PrefetchScalarGridSpec(
            num_scalar_prefetch=1,
            grid=(blocks,),
            in_specs=[part(0), part(1), part(2), part(3),
                      pl.BlockSpec((CHUNK, 1), lambda i, s: (i, 0)),
                      pl.BlockSpec((1, CHUNK), lambda i, s: (0, i)),
                      pl.BlockSpec((1, HD), lambda i, s: (0, 0))],
            out_specs=[pl.BlockSpec((CHUNK, width), lambda i, s: (i, 0)),
                       pl.BlockSpec((CHUNK, width), lambda i, s: (i, 0)),
                       pl.BlockSpec((1, HD, width), lambda i, s: (i, 0, 0))],
            scratch_shapes=[pltpu.VMEM((HD, width), F32)],
        ),
        out_shape=[jax.ShapeDtypeStruct((length, width), BF16),
                   jax.ShapeDtypeStruct((length, width), F32),
                   jax.ShapeDtypeStruct((blocks, HD, width), F32)],
        cost_estimate=pl.CostEstimate(flops=30_000_000_000, bytes_accessed=10_000_000, transcendentals=0),
        name="mixer_forward",
    )(seg, proj, proj, proj, proj, seg.reshape(length, 1), seg.reshape(1, length), gain.reshape(1, HD))


def rec_backward(proj, seg, gain, o, states, dy):
    length, width = proj.shape[0], proj.shape[1] // 4
    blocks = length // CHUNK
    last = blocks - 1
    part = lambda k: pl.BlockSpec((CHUNK, width), lambda i, s, k=k: (last - i, k))
    return pl.pallas_call(
        backward_kernel,
        grid_spec=pltpu.PrefetchScalarGridSpec(
            num_scalar_prefetch=1,
            grid=(blocks,),
            in_specs=[part(0), part(1), part(2), part(3),
                      pl.BlockSpec((CHUNK, 1), lambda i, s: (last - i, 0)),
                      pl.BlockSpec((1, CHUNK), lambda i, s: (0, last - i)),
                      pl.BlockSpec((1, HD), lambda i, s: (0, 0)),
                      part(0),
                      pl.BlockSpec((1, HD, width), lambda i, s: (last - i, 0, 0)),
                      part(0)],
            out_specs=[pl.BlockSpec((CHUNK, 4 * width), lambda i, s: (last - i, 0)),
                       pl.BlockSpec((1, HD), lambda i, s: (0, 0))],
            scratch_shapes=[pltpu.VMEM((HD, width), F32)],
        ),
        out_shape=[jax.ShapeDtypeStruct((length, 4 * width), BF16),
                   jax.ShapeDtypeStruct((1, HD), F32)],
        cost_estimate=pl.CostEstimate(flops=60_000_000_000, bytes_accessed=14_000_000, transcendentals=0),
        name="mixer_backward",
    )(seg, proj, proj, proj, proj, seg.reshape(length, 1), seg.reshape(1, length), gain.reshape(1, HD), o, states, dy)


EPSILON = 1e-06
SPEC_ROWS = P(("dp", "tensor"), None)


def ring_order(count):
    return list(range(0, count, 2)) + list(range(count - 1 - count % 2, 0, -2))


class Ring:
    def __init__(self, axis, count):
        order = ring_order(count)
        self.axis, self.count = axis, count
        self.ahead = [(order[i], order[(i + 1) % count]) for i in range(count)]
        self.behind = [(b, a) for a, b in self.ahead]
        self.me = lax.axis_index(axis)
        self.place = jnp.where(self.me % 2 == 0, self.me // 2, count - (self.me + 1) // 2)

    def owner(self, shift):
        at = (self.place + shift + 2 * self.count) % self.count
        return jnp.where(2 * at < self.count, 2 * at, 2 * (self.count - at) - 1)

    def send_ahead(self, x):
        return lax.ppermute(x, self.axis, self.ahead)

    def send_behind(self, x):
        return lax.ppermute(x, self.axis, self.behind)

    def gather(self, x, dim):
        return Gather(self, x, dim)

    def scatter_sum(self, x, dim):
        return ScatterSum(self, x, dim)


def after(x, *earlier):
    return lax.optimization_barrier((x, *earlier))[0]


def first_kernel(at, block, whole):
    whole[...] = block[...]


def pair_kernel(at, left, right, before, whole):
    @pl.when(pl.program_id(0) == 0)
    def _():
        whole[...] = left[...]

    @pl.when(pl.program_id(0) == 1)
    def _():
        whole[...] = right[...]


SMALL_COST = pl.CostEstimate(flops=0, bytes_accessed=4_000_000, transcendentals=0)


class Gather:
    def __init__(self, ring, x, dim):
        self.ring, self.dim, self.half = ring, dim, x.shape[0] // 2
        shape = list(x.shape)
        shape[dim] *= ring.count
        self.shape = jax.ShapeDtypeStruct(tuple(shape), x.dtype)
        self.left = self.right = x
        self.step, self.steps = 0, ring.count // 2
        self.aligned = x.shape[1] % 128 == 0
        if not self.aligned:
            at = [0, 0]
            at[dim] = ring.me * x.shape[dim]
            self.whole = lax.dynamic_update_slice(jnp.zeros(shape, x.dtype), x, at)
            return
        to = (lambda i, at: (at[0], 0)) if self.dim == 0 else (lambda i, at: (0, at[0]))
        self.whole = pl.pallas_call(
            first_kernel,
            grid_spec=pltpu.PrefetchScalarGridSpec(
                num_scalar_prefetch=1, grid=(1,), in_specs=[pl.BlockSpec(x.shape, lambda i, at: (0, 0))],
                out_specs=pl.BlockSpec(x.shape, to)),
            out_shape=self.shape, cost_estimate=SMALL_COST, name="gather_first",
        )(self.ring.me.reshape(1), x)

    def hop(self, *earlier):
        ring = self.ring
        left, right = self.left, self.right
        if self.step == self.steps:
            return left, right
        step = self.step + 1
        if step == self.steps:
            left, right = left[: self.half], right[self.half :]
        if step > 1:
            left, right, self.whole, *_ = lax.optimization_barrier((left, right, self.whole, *earlier))
        elif earlier:
            left, right = after(left, *earlier), after(right, *earlier)
        left, right = ring.send_ahead(left), ring.send_behind(right)
        if step > 1:
            self.store()
        self.left, self.right, self.step = left, right, step
        return left, right

    def settle(self, x):
        x, self.whole = lax.optimization_barrier((x, self.whole))
        return x

    def result(self):
        while self.step < self.steps:
            self.hop()
        self.store()
        return self.whole

    def store(self):
        ring = self.ring
        last = self.step == self.steps
        if not self.aligned:
            for block, shift in ((self.left, -self.step), (self.right, self.step)):
                at = [self.half if last and shift > 0 else 0, 0]
                at[self.dim] = at[self.dim] + ring.owner(shift) * self.shape.shape[self.dim] // ring.count
                self.whole = lax.dynamic_update_slice(self.whole, block, at)
            return
        owners = jnp.stack([ring.owner(-self.step), ring.owner(self.step)])
        if self.dim == 0 and last:
            to = lambda i, at: (2 * at[i] + i, 0)
        elif self.dim == 0:
            to = lambda i, at: (at[i], 0)
        elif last:
            to = lambda i, at: (i, at[i])
        else:
            to = lambda i, at: (0, at[i])
        block = pl.BlockSpec(self.left.shape, lambda i, at: (0, 0))
        self.whole = pl.pallas_call(
            pair_kernel,
            grid_spec=pltpu.PrefetchScalarGridSpec(
                num_scalar_prefetch=1, grid=(2,),
                in_specs=[block, block, pl.BlockSpec(memory_space=pl.ANY)],
                out_specs=pl.BlockSpec(self.left.shape, to)),
            out_shape=self.shape, input_output_aliases={3: 0}, cost_estimate=SMALL_COST, name="gather_pair",
        )(owners, self.left, self.right, self.whole)


class ScatterSum:
    def __init__(self, ring, x, dim):
        self.ring, self.dim, self.x = ring, dim, x
        shape = list(x.shape)
        shape[dim] //= ring.count
        self.size, self.half = shape[dim], shape[0] // 2
        self.shape, self.step, self.steps = shape, 0, ring.count // 2
        self.left = self.part(self.steps)[: self.half]
        self.right = self.part(-self.steps)[self.half :]

    def part(self, shift):
        at = [0, 0]
        at[self.dim] = self.ring.owner(shift) * self.size
        return lax.dynamic_slice(self.x, at, self.shape)

    def hop(self, before=(), during=()):
        ring, left, right = self.ring, self.left, self.right
        if self.step == self.steps:
            return self.arrived
        self.step += 1
        if before:
            left, right = after(left, *before), after(right, *before)
        left, right = ring.send_ahead(left), ring.send_behind(right)
        if during:
            left, right = after(left, *during), after(right, *during)
        self.arrived = left, right
        shift = self.steps - self.step
        if self.step == 1:
            ahead, behind = self.part(shift), self.part(-shift)
            self.left = jnp.concatenate([left + ahead[: self.half], ahead[self.half :]], axis=0)
            self.right = jnp.concatenate([behind[: self.half], right + behind[self.half :]], axis=0)
        elif shift:
            self.left, self.right = left + self.part(shift), right + self.part(-shift)
        return self.arrived

    def result(self):
        while self.step < self.steps:
            self.hop()
        left, right = self.arrived
        return left.astype(F32) + right.astype(F32) + self.part(0).astype(F32)


def gather_small(row, axis, count):
    me = lax.axis_index(axis)
    whole = lax.dynamic_update_slice(jnp.zeros((count, row.shape[1]), row.dtype), row, (me, 0))
    for turn in range(1, count):
        got = lax.ppermute(row, axis, [(i, (i + turn) % count) for i in range(count)])
        whole = lax.dynamic_update_slice(whole, got, ((me - turn + count) % count, 0))
    return whole


def scatter_sum_small(rows, axis, count):
    me = lax.axis_index(axis)
    total = lax.dynamic_slice_in_dim(rows, me, 1, 0)
    for turn in range(1, count):
        mine = lax.dynamic_slice_in_dim(rows, (me + turn) % count, 1, 0)
        total = total + lax.ppermute(mine, axis, [(i, (i + turn) % count) for i in range(count)])
    return total


def norm_forward(values, gain):
    r = lax.rsqrt(jnp.mean(values * values, axis=-1, keepdims=True) + EPSILON)
    return (values * r * gain).astype(BF16), r


def norm_backward(values, r, gain, grad):
    n = values * r
    scaled = grad * gain
    back = r * (scaled - n * jnp.mean(scaled * n, axis=-1, keepdims=True))
    return back, jnp.sum(grad * n, axis=0)


def tensor_gather(x):
    return lax.all_gather(x, "tensor", axis=0, tiled=True)


def tensor_scatter_sum(x):
    return lax.psum_scatter(x, "tensor", scatter_dimension=0, tiled=True).astype(F32)


def body(n_dp, n_tensor, tokens, segment_ids, mixer_in, mixer_out, gate_up, down,
         norm_gain, group_gain, ffn_gain, cotangent):
    ring = Ring("dp", n_dp)
    seg = segment_ids[0]
    part, small = norm_gain.shape[0], group_gain.shape[0]
    model = part * n_dp
    width = mixer_out.shape[0]
    hidden_width = down.shape[0]

    gain_row = jnp.concatenate([norm_gain, ffn_gain, group_gain]).astype(F32)[None]
    in_part = mixer_in.reshape(part, 4 * width)
    gu_part = gate_up.reshape(part, 2 * hidden_width)
    seq = tensor_gather(tokens)
    cot = tensor_gather(cotangent)
    gains = gather_small(gain_row, "dp", n_dp)
    gain_in = gains[:, :part].reshape(1, model)
    gain_ffn = gains[:, part : 2 * part].reshape(1, model)
    gain_group = gains[:, 2 * part :].reshape(1, HD)

    g_in, g_out = ring.gather(in_part, 0), ring.gather(mixer_out, 1)
    done = g_out.hop()
    done = g_in.hop(*done)
    done = g_out.hop(*done)
    done = g_in.hop(*done)
    g_gu, g_down = ring.gather(gu_part, 0), ring.gather(down, 1)
    done = g_out.hop(*done, gains)
    h1, _ = norm_forward(after(seq, *done).astype(F32), gain_in)
    done = g_in.hop(*done)
    h1, g_gu.whole, g_down.whole = lax.optimization_barrier((h1, g_gu.whole, g_down.whole))
    done = g_out.hop(*done, h1)
    done = g_in.hop(*done)
    w_in, w_out = g_in.result(), g_out.result()

    gu1 = g_gu.hop(*done)
    proj = mm(h1, w_in, NN).astype(BF16)
    y, o, states = rec_forward(proj, seg, gain_group)
    attn_part = after(mm(y, w_out, NN).astype(BF16), *gu1)
    gu2 = g_gu.hop(attn_part)
    down1 = g_down.hop(attn_part)
    attn = tensor_scatter_sum(attn_part)
    x = tokens.astype(F32)
    x2 = x + g_gu.settle(after(attn, *gu2, *down1))
    h2_own, r2 = norm_forward(x2, gain_ffn)
    gu3 = g_gu.hop(*down1)
    h2 = g_gu.settle(after(tensor_gather(h2_own), *gu3))
    gu4 = g_gu.hop()
    down2 = g_down.hop(*gu4)
    w_gu = g_gu.result()
    gu = after(mm(h2, w_gu, NN), *down2)
    down3 = g_down.hop(gu)
    gate, up = gu[:, :hidden_width], gu[:, hidden_width:]
    sg = jax.nn.sigmoid(gate)
    swish = gate * sg
    hidden = (swish * up).astype(BF16)
    d_down_part = g_down.settle(mm(hidden, cot, TN).astype(BF16))
    s_down = ring.scatter_sum(d_down_part, 1)
    step1 = s_down.hop()
    down4 = g_down.hop(d_down_part)
    w_down = g_down.result()
    dh = mm(after(cot, d_down_part, *step1), w_down, NT)
    dgate = (dh * up * sg * (1.0 + gate * (1.0 - sg))).astype(BF16)
    dup = (dh * swish).astype(BF16)
    dgu = jnp.concatenate([dgate, dup], axis=1)
    s_down.hop(during=(dgu,))
    d_gu_part = mm(after(h2, s_down.left, s_down.right), dgu, TN).astype(BF16)
    s_down.hop(during=(d_gu_part,))
    s_gu = ring.scatter_sum(d_gu_part, 0)
    dh2_part = mm(after(dgu, d_gu_part, s_down.left, s_down.right), w_gu, NT).astype(BF16)
    step4 = s_down.hop(during=(dh2_part,))
    t1 = s_gu.hop(during=(dh2_part,))
    dh2_part = after(dh2_part, *step4, *t1)
    dh2 = tensor_scatter_sum(dh2_part)
    s_gu.hop()
    d_down = after(s_down.result(), dh2_part)
    back2, d_gain_ffn = norm_backward(x2, r2, gain_ffn, after(dh2, s_gu.left, s_gu.right, d_down))
    dx2 = cotangent.astype(F32) + back2
    dattn_own = dx2.astype(BF16)
    dattn = tensor_gather(dattn_own)
    ffn_part = mm(after(hidden, dattn_own), w_down, NN).astype(BF16)
    s_gu.hop(during=(ffn_part,))
    dattn = after(dattn, s_gu.left, s_gu.right)
    d_out_part = mm(y, dattn, TN).astype(BF16)
    s_out = ring.scatter_sum(d_out_part, 1)
    ffn = tensor_scatter_sum(after(ffn_part, dattn))
    dy = mm(after(dattn, d_out_part), w_out, NT)
    dproj, d_group = rec_backward(proj, seg, gain_group, o, states, dy)
    t4 = s_gu.hop(during=(dproj,))
    s_out.hop(during=(dproj,))
    dproj = after(dproj, *t4, s_out.left, s_out.right)
    s_qa = ring.scatter_sum(mm(h1, dproj[:, : 2 * width], TN).astype(BF16), 0)
    s_out.hop(during=(s_qa.x,))
    dh1_part = mm(after(dproj, s_qa.x, s_out.left, s_out.right), w_in, NT).astype(BF16)
    s_out.hop(during=(dh1_part,))
    s_qa.hop(during=(dh1_part,))
    dh1_part = after(dh1_part, s_out.left, s_out.right, s_qa.left, s_qa.right)
    dh1 = tensor_scatter_sum(dh1_part)
    s_vz = ring.scatter_sum(mm(after(h1, dh1_part), dproj[:, 2 * width :], TN).astype(BF16), 0)
    d_gate_up = after(s_gu.result(), s_vz.x)
    d_gu = d_gate_up.reshape(part, 2, hidden_width)
    s_out.hop(during=(s_vz.x,))
    s_qa.hop(during=(s_vz.x, d_gu))
    d_out = s_out.result()
    s_vz.hop(during=(d_out,))
    output = after((x2 + ffn).astype(BF16), s_qa.left, s_vz.left)
    s_qa.hop(during=(output,))
    s_vz.hop(during=(output,))
    r1 = lax.rsqrt(jnp.mean(x * x, axis=-1, keepdims=True) + EPSILON)
    back1, d_gain_in = norm_backward(x, r1, gain_in, after(dh1, s_qa.left, s_qa.right, s_vz.left, s_vz.right))
    d_tokens = (dx2 + back1).astype(BF16)
    d_gains = jnp.concatenate(
        [d_gain_in.reshape(n_dp, part), d_gain_ffn.reshape(n_dp, part), d_group.reshape(n_dp, small)], axis=1
    )
    d_gains = lax.psum(d_gains, "tensor")
    qa4 = s_qa.hop(during=(d_gains,))
    s_vz.hop(during=(d_gains,))
    d_gains = scatter_sum_small(after(d_gains, *qa4, s_vz.left, s_vz.right), "dp", n_dp)[0]
    d_qa = s_qa.result().reshape(part, 2, width)
    s_vz.hop(during=(d_qa,))
    d_in = jnp.concatenate([d_qa, s_vz.result().reshape(part, 2, width)], axis=1)
    return (
        output,
        d_tokens,
        d_in,
        d_out,
        d_gu,
        d_down,
        d_gains[:part],
        d_gains[2 * part :],
        d_gains[part : 2 * part],
    )


def solution(mesh):
    split = P("dp", None, "tensor")
    cross = P("tensor", "dp")
    return jax.shard_map(
        functools.partial(body, mesh.shape["dp"], mesh.shape["tensor"]),
        mesh=mesh,
        in_specs=(SPEC_ROWS, P("dp", None), split, cross, split, cross, P("dp"), P("dp"), P("dp"), SPEC_ROWS),
        out_specs=(SPEC_ROWS, SPEC_ROWS, split, cross, split, cross, P("dp"), P("dp"), P("dp")),
        check_vma=False,
    )
```

```python
import functools
import jax
import jax.numpy as jnp
from jax import lax
from jax.experimental import pallas as pl
from jax.experimental.pallas import tpu as pltpu
from jax.sharding import PartitionSpec as P

HD = 128
CHUNK = 128
GROUP_EPSILON = 0.01
F32 = jnp.float32
BF16 = jnp.bfloat16
NN = (((1,), (0,)), ((), ()))
NT = (((1,), (1,)), ((), ()))
TN = (((0,), (0,)), ((), ()))


def mm(a, b, dims):
    return lax.dot_general(a, b, dims, preferred_element_type=F32)


def halves(x):
    high = x.astype(BF16)
    return high, (x - high.astype(F32)).astype(BF16)


def tri_sum(tri, x):
    high, rest = halves(x)
    return mm(tri, high, NN) + mm(tri, rest, NN)


def decays(a_raw, lower):
    sig = jax.nn.sigmoid(a_raw)
    forget = 0.8 + 0.2 * sig
    key = 1.0 - forget
    cum = tri_sum(lower, jnp.log(forget))
    return sig, forget, key, cum


def masks(seg, doc_col, doc_row, block):
    rows = lax.broadcasted_iota(jnp.int32, (CHUNK, CHUNK), 0)
    cols = lax.broadcasted_iota(jnp.int32, (CHUNK, CHUNK), 1)
    causal = rows >= cols
    same = jnp.logical_and(causal, doc_col == doc_row)
    start = block * CHUNK
    end_doc = seg[start + CHUNK - 1]
    last_doc = jnp.where(block > 0, seg[jnp.maximum(start - 1, 0)], -1)
    cont = (doc_col == last_doc).astype(F32)
    tail = (doc_col == end_doc).astype(F32)
    keep = jnp.where(end_doc == last_doc, 1.0, 0.0).astype(F32)
    return causal, same, cont, tail, keep


def forward_kernel(seg, q_ref, a_ref, v_ref, z_ref, col_ref, row_ref, gain_ref,
                   y_ref, o_ref, s_ref, state):
    block = pl.program_id(0)

    @pl.when(block == 0)
    def _():
        state[...] = jnp.zeros_like(state)

    width = q_ref.shape[1]
    causal, same, cont, tail, keep = masks(seg, col_ref[...], row_ref[...], block)
    lower = jnp.where(causal, 1.0, 0.0).astype(BF16)
    _, _, key, cum = decays(a_ref[...].astype(F32), lower)
    total = cum[CHUNK - 1 : CHUNK, :]
    qd, qd_rest = halves(q_ref[...].astype(F32) * jnp.exp(cum))
    kd, kd_rest = halves(key * jnp.exp(-cum))
    kt, kt_rest = halves(key * jnp.exp(total - cum) * tail)
    fade = jnp.exp(total) * keep
    gain = gain_ref[...]
    s_ref[0] = state[...]
    for head in range(width // HD):
        at = slice(head * HD, (head + 1) * HD)
        v = v_ref[:, at]
        st = state[:, at]
        st_high, st_rest = halves(st)
        qh, ql = qd[:, at], qd_rest[:, at]
        scores = mm(qh, kd[:, at], NT) + (mm(qh, kd_rest[:, at], NT) + mm(ql, kd[:, at], NT))
        scores = jnp.where(same, scores, 0.0).astype(BF16)
        earlier = mm(qh, st_high, NT) + (mm(qh, st_rest, NT) + mm(ql, st_high, NT))
        o = mm(scores, v, NN) + cont * earlier
        state[:, at] = st * fade[:, at] + (mm(v, kt[:, at], TN) + mm(v, kt_rest[:, at], TN))
        o_ref[:, at] = o
        z = z_ref[:, at].astype(F32)
        r = lax.rsqrt(jnp.mean(o * o, axis=-1, keepdims=True) + GROUP_EPSILON)
        y_ref[:, at] = (o * r * gain * (z * jax.nn.sigmoid(z))).astype(BF16)


def backward_kernel(seg, q_ref, a_ref, v_ref, z_ref, col_ref, row_ref, gain_ref, o_ref, s_ref, dy_ref,
                    d_ref, dgain_ref, dstate):
    step = pl.program_id(0)
    block = pl.num_programs(0) - 1 - step

    @pl.when(step == 0)
    def _():
        dstate[...] = jnp.zeros_like(dstate)
        dgain_ref[...] = jnp.zeros_like(dgain_ref)

    width = q_ref.shape[1]
    causal, same, cont, tail, keep = masks(seg, col_ref[...], row_ref[...], block)
    lower = jnp.where(causal, 1.0, 0.0).astype(BF16)
    sig, forget, key, cum = decays(a_ref[...].astype(F32), lower)
    total = cum[CHUNK - 1 : CHUNK, :]
    up = jnp.exp(cum)
    down = jnp.exp(-cum)
    late = jnp.exp(total - cum) * tail
    qd = (q_ref[...].astype(F32) * up).astype(BF16)
    kd = (key * down).astype(BF16)
    kt = (key * late).astype(BF16)
    fade = jnp.exp(total) * keep
    gain = gain_ref[...]
    gain_sum = jnp.zeros((1, HD), F32)
    dcums = []
    dkeys = []
    for head in range(width // HD):
        at = slice(head * HD, (head + 1) * HD)
        v = v_ref[:, at]
        o = o_ref[:, at]
        z = z_ref[:, at].astype(F32)
        dy = dy_ref[:, at]
        r = lax.rsqrt(jnp.mean(o * o, axis=-1, keepdims=True) + GROUP_EPSILON)
        n = o * r
        sz = jax.nn.sigmoid(z)
        dng = dy * (z * sz)
        gain_sum += jnp.sum(dng * n, axis=0, keepdims=True)
        dn = dng * gain
        do = (r * (dn - n * jnp.mean(dn * n, axis=-1, keepdims=True))).astype(BF16)
        d_ref[:, 3 * width + head * HD : 3 * width + (head + 1) * HD] = (
            dy * n * gain * (sz * (1.0 + z * (1.0 - sz)))
        ).astype(BF16)
        qh, kh, th = qd[:, at], kd[:, at], kt[:, at]
        scores = jnp.where(same, mm(qh, kh, NT), 0.0).astype(BF16)
        dscores = jnp.where(same, mm(do, v, NT), 0.0).astype(BF16)
        st = s_ref[0, :, at]
        dst = dstate[:, at]
        dst_low = dst.astype(BF16)
        dv = mm(scores, do, TN) + mm(th, dst_low, NT)
        dqd = mm(dscores, kh, NN) + cont * mm(do, st.astype(BF16), NN)
        dkd = mm(dscores, qh, TN)
        dkt = mm(v, dst_low, NN)
        carried = dkt * th.astype(F32)
        dtotal = jnp.sum(carried, axis=0, keepdims=True) + fade[:, at] * jnp.sum(
            dst * st, axis=0, keepdims=True
        )
        dstate[:, at] = dst * fade[:, at] + mm((do.astype(F32) * cont).astype(BF16), qh, TN)
        d_ref[:, head * HD : (head + 1) * HD] = (dqd * up[:, at]).astype(BF16)
        d_ref[:, 2 * width + head * HD : 2 * width + (head + 1) * HD] = dv.astype(BF16)
        dkeys.append(dkd * down[:, at] + dkt * late[:, at])
        dcum = dqd * qh.astype(F32) - dkd * kh.astype(F32) - carried
        high, rest = halves(dcum)
        dlog = mm(lower, high, TN) + mm(lower, rest, TN) + dtotal
        slope = 0.2 * sig[:, at] * (1.0 - sig[:, at])
        d_ref[:, width + head * HD : width + (head + 1) * HD] = (
            (dlog / forget[:, at] - dkeys[-1]) * slope
        ).astype(BF16)
    dgain_ref[...] += gain_sum


def rec_forward(proj, seg, gain):
    length, width = proj.shape[0], proj.shape[1] // 4
    blocks = length // CHUNK
    part = lambda k: pl.BlockSpec((CHUNK, width), lambda i, s, k=k: (i, k))
    return pl.pallas_call(
        forward_kernel,
        grid_spec=pltpu.PrefetchScalarGridSpec(
            num_scalar_prefetch=1,
            grid=(blocks,),
            in_specs=[part(0), part(1), part(2), part(3),
                      pl.BlockSpec((CHUNK, 1), lambda i, s: (i, 0)),
                      pl.BlockSpec((1, CHUNK), lambda i, s: (0, i)),
                      pl.BlockSpec((1, HD), lambda i, s: (0, 0))],
            out_specs=[pl.BlockSpec((CHUNK, width), lambda i, s: (i, 0)),
                       pl.BlockSpec((CHUNK, width), lambda i, s: (i, 0)),
                       pl.BlockSpec((1, HD, width), lambda i, s: (i, 0, 0))],
            scratch_shapes=[pltpu.VMEM((HD, width), F32)],
        ),
        out_shape=[jax.ShapeDtypeStruct((length, width), BF16),
                   jax.ShapeDtypeStruct((length, width), F32),
                   jax.ShapeDtypeStruct((blocks, HD, width), F32)],
        cost_estimate=pl.CostEstimate(flops=30_000_000_000, bytes_accessed=10_000_000, transcendentals=0),
        name="mixer_forward",
    )(seg, proj, proj, proj, proj, seg.reshape(length, 1), seg.reshape(1, length), gain.reshape(1, HD))


def rec_backward(proj, seg, gain, o, states, dy):
    length, width = proj.shape[0], proj.shape[1] // 4
    blocks = length // CHUNK
    last = blocks - 1
    part = lambda k: pl.BlockSpec((CHUNK, width), lambda i, s, k=k: (last - i, k))
    return pl.pallas_call(
        backward_kernel,
        grid_spec=pltpu.PrefetchScalarGridSpec(
            num_scalar_prefetch=1,
            grid=(blocks,),
            in_specs=[part(0), part(1), part(2), part(3),
                      pl.BlockSpec((CHUNK, 1), lambda i, s: (last - i, 0)),
                      pl.BlockSpec((1, CHUNK), lambda i, s: (0, last - i)),
                      pl.BlockSpec((1, HD), lambda i, s: (0, 0)),
                      part(0),
                      pl.BlockSpec((1, HD, width), lambda i, s: (last - i, 0, 0)),
                      part(0)],
            out_specs=[pl.BlockSpec((CHUNK, 4 * width), lambda i, s: (last - i, 0)),
                       pl.BlockSpec((1, HD), lambda i, s: (0, 0))],
            scratch_shapes=[pltpu.VMEM((HD, width), F32)],
        ),
        out_shape=[jax.ShapeDtypeStruct((length, 4 * width), BF16),
                   jax.ShapeDtypeStruct((1, HD), F32)],
        cost_estimate=pl.CostEstimate(flops=60_000_000_000, bytes_accessed=14_000_000, transcendentals=0),
        name="mixer_backward",
    )(seg, proj, proj, proj, proj, seg.reshape(length, 1), seg.reshape(1, length), gain.reshape(1, HD), o, states, dy)


EPSILON = 1e-06
SPEC_ROWS = P(("dp", "tensor"), None)


def ring_order(count):
    return list(range(0, count, 2)) + list(range(count - 1 - count % 2, 0, -2))


class Ring:
    def __init__(self, axis, count):
        order = ring_order(count)
        self.axis, self.count = axis, count
        self.ahead = [(order[i], order[(i + 1) % count]) for i in range(count)]
        self.behind = [(b, a) for a, b in self.ahead]
        self.me = lax.axis_index(axis)
        self.place = jnp.where(self.me % 2 == 0, self.me // 2, count - (self.me + 1) // 2)

    def owner(self, shift):
        at = (self.place + shift + 2 * self.count) % self.count
        return jnp.where(2 * at < self.count, 2 * at, 2 * (self.count - at) - 1)

    def send_ahead(self, x):
        return lax.ppermute(x, self.axis, self.ahead)

    def send_behind(self, x):
        return lax.ppermute(x, self.axis, self.behind)

    def gather(self, x, dim):
        return Gather(self, x, dim)

    def scatter_sum(self, x, dim):
        return ScatterSum(self, x, dim)


def after(x, *earlier):
    return lax.optimization_barrier((x, *earlier))[0]


def first_kernel(at, block, whole):
    whole[...] = block[...]


def pair_kernel(at, left, right, before, whole):
    @pl.when(pl.program_id(0) == 0)
    def _():
        whole[...] = left[...]

    @pl.when(pl.program_id(0) == 1)
    def _():
        whole[...] = right[...]


SMALL_COST = pl.CostEstimate(flops=0, bytes_accessed=4_000_000, transcendentals=0)


class Gather:
    def __init__(self, ring, x, dim):
        self.ring, self.dim, self.half = ring, dim, x.shape[0] // 2
        shape = list(x.shape)
        shape[dim] *= ring.count
        self.shape = jax.ShapeDtypeStruct(tuple(shape), x.dtype)
        self.left = self.right = x
        self.step, self.steps, self.pending = 0, ring.count // 2, False
        self.aligned = x.shape[1] % 128 == 0
        if not self.aligned:
            at = [0, 0]
            at[dim] = ring.me * x.shape[dim]
            self.whole = lax.dynamic_update_slice(jnp.zeros(shape, x.dtype), x, at)
            return
        to = (lambda i, at: (at[0], 0)) if self.dim == 0 else (lambda i, at: (0, at[0]))
        self.whole = pl.pallas_call(
            first_kernel,
            grid_spec=pltpu.PrefetchScalarGridSpec(
                num_scalar_prefetch=1, grid=(1,), in_specs=[pl.BlockSpec(x.shape, lambda i, at: (0, 0))],
                out_specs=pl.BlockSpec(x.shape, to)),
            out_shape=self.shape, cost_estimate=SMALL_COST, name="gather_first",
        )(self.ring.me.reshape(1), x)

    def hop(self, *earlier):
        ring = self.ring
        left, right = self.left, self.right
        if self.step == self.steps:
            return left, right
        step = self.step + 1
        if step == self.steps:
            left, right = left[: self.half], right[self.half :]
        if step > 1:
            left, right, self.whole, *_ = lax.optimization_barrier((left, right, self.whole, *earlier))
        elif earlier:
            left, right, *_ = lax.optimization_barrier((left, right, *earlier))
        left, right = ring.send_ahead(left), ring.send_behind(right)
        if step > 1:
            self.store()
        self.left, self.right, self.step, self.pending = left, right, step, True
        return left, right

    def halves(self):
        if self.step + 1 == self.steps:
            return self.left[: self.half], self.right[self.half :]
        return self.left, self.right

    def send(self, left, right):
        left, right = self.ring.send_ahead(left), self.ring.send_behind(right)
        self.store()
        self.left, self.right, self.step, self.pending = left, right, self.step + 1, True

    def settle(self, x):
        x, self.whole = lax.optimization_barrier((x, self.whole))
        return x

    def result(self):
        while self.step < self.steps:
            self.hop()
        self.store()
        return self.whole

    def store(self):
        if not self.pending:
            return
        self.pending = False
        ring = self.ring
        last = self.step == self.steps
        if not self.aligned:
            for block, shift in ((self.left, -self.step), (self.right, self.step)):
                at = [self.half if last and shift > 0 else 0, 0]
                at[self.dim] = at[self.dim] + ring.owner(shift) * self.shape.shape[self.dim] // ring.count
                self.whole = lax.dynamic_update_slice(self.whole, block, at)
            return
        owners = jnp.stack([ring.owner(-self.step), ring.owner(self.step)])
        if self.dim == 0 and last:
            to = lambda i, at: (2 * at[i] + i, 0)
        elif self.dim == 0:
            to = lambda i, at: (at[i], 0)
        elif last:
            to = lambda i, at: (i, at[i])
        else:
            to = lambda i, at: (0, at[i])
        block = pl.BlockSpec(self.left.shape, lambda i, at: (0, 0))
        self.whole = pl.pallas_call(
            pair_kernel,
            grid_spec=pltpu.PrefetchScalarGridSpec(
                num_scalar_prefetch=1, grid=(2,),
                in_specs=[block, block, pl.BlockSpec(memory_space=pl.ANY)],
                out_specs=pl.BlockSpec(self.left.shape, to)),
            out_shape=self.shape, input_output_aliases={3: 0}, cost_estimate=SMALL_COST, name="gather_pair",
        )(owners, self.left, self.right, self.whole)


def hop_together(one, two):
    if one.step == one.steps:
        return
    blocks = *one.halves(), *two.halves()
    if one.step:
        *blocks, one.whole, two.whole = lax.optimization_barrier((*blocks, one.whole, two.whole))
    one.send(*blocks[:2])
    two.send(*blocks[2:])


class ScatterSum:
    def __init__(self, ring, x, dim):
        self.ring, self.dim, self.x = ring, dim, x
        shape = list(x.shape)
        shape[dim] //= ring.count
        self.size, self.half = shape[dim], shape[0] // 2
        self.shape, self.step, self.steps = shape, 0, ring.count // 2
        self.left = self.part(self.steps)[: self.half]
        self.right = self.part(-self.steps)[self.half :]

    def part(self, shift):
        at = [0, 0]
        at[self.dim] = self.ring.owner(shift) * self.size
        return lax.dynamic_slice(self.x, at, self.shape)

    def hop(self, before=(), during=()):
        ring, left, right = self.ring, self.left, self.right
        if self.step == self.steps:
            return self.arrived
        self.step += 1
        left, right, *_ = lax.optimization_barrier((left, right, *before))
        left, right = ring.send_ahead(left), ring.send_behind(right)
        left, right, *_ = lax.optimization_barrier((left, right, *during))
        self.arrived = left, right
        shift = self.steps - self.step
        if self.step == 1:
            ahead, behind = self.part(shift), self.part(-shift)
            rest, zero = ahead.shape[0] - self.half, jnp.zeros((), left.dtype)
            self.left = lax.pad(left, zero, ((0, rest, 0), (0, 0, 0))) + ahead
            self.right = lax.pad(right, zero, ((self.half, 0, 0), (0, 0, 0))) + behind
        elif shift:
            self.left, self.right = left + self.part(shift), right + self.part(-shift)
        return self.arrived

    def result(self):
        while self.step < self.steps:
            self.hop()
        left, right = self.arrived
        return left.astype(F32) + right.astype(F32) + self.part(0).astype(F32)


def gather_small(row, axis, count):
    me = lax.axis_index(axis)
    whole = lax.dynamic_update_slice(jnp.zeros((count, row.shape[1]), row.dtype), row, (me, 0))
    for turn in range(1, count):
        got = lax.ppermute(row, axis, [(i, (i + turn) % count) for i in range(count)])
        whole = lax.dynamic_update_slice(whole, got, ((me - turn + count) % count, 0))
    return whole


def scatter_sum_small(rows, axis, count):
    me = lax.axis_index(axis)
    if count & (count - 1):
        return lax.dynamic_slice_in_dim(lax.psum(rows, axis), me, 1, 0)
    while count > 1:
        count //= 2
        side = me // count % 2
        mine = lax.dynamic_slice_in_dim(rows, side * count, count, 0)
        other = lax.dynamic_slice_in_dim(rows, (1 - side) * count, count, 0)
        whole = lax.axis_size(axis)
        rows = mine + lax.ppermute(other, axis, [(i, i ^ count) for i in range(whole)])
    return rows


def norm_forward(values, gain):
    r = lax.rsqrt(jnp.mean(values * values, axis=-1, keepdims=True) + EPSILON)
    return (values * r * gain).astype(BF16), r


def norm_backward(values, r, gain, grad):
    n = values * r
    scaled = grad * gain
    back = r * (scaled - n * jnp.mean(scaled * n, axis=-1, keepdims=True))
    return back, jnp.sum(grad * n, axis=0)


def tensor_gather(x):
    return lax.all_gather(x, "tensor", axis=0, tiled=True)


def tensor_scatter_sum(x):
    return lax.psum_scatter(x, "tensor", scatter_dimension=0, tiled=True).astype(F32)


def body(n_dp, n_tensor, tokens, segment_ids, mixer_in, mixer_out, gate_up, down,
         norm_gain, group_gain, ffn_gain, cotangent):
    ring = Ring("dp", n_dp)
    seg = segment_ids[0]
    part, small = norm_gain.shape[0], group_gain.shape[0]
    model = part * n_dp
    width = mixer_out.shape[0]
    hidden_width = down.shape[0]

    in_part = mixer_in.reshape(part, 4 * width)
    gu_part = gate_up.reshape(part, 2 * hidden_width)
    extra = 32
    gain_rows = jnp.concatenate([norm_gain, ffn_gain, group_gain])
    gain_rows = jnp.pad(gain_rows, (0, extra * mixer_out.shape[1] - gain_rows.shape[0]))
    out_part = jnp.concatenate([mixer_out, gain_rows.reshape(extra, mixer_out.shape[1])], axis=0)
    seq = tensor_gather(tokens)
    cot = tensor_gather(cotangent)

    g_in, g_out = ring.gather(in_part, 0), ring.gather(out_part, 1)
    hop_together(g_out, g_in)
    g_gu, g_down = ring.gather(gu_part, 0), ring.gather(down, 1)
    hop_together(g_out, g_in)
    g_in.left, g_gu.whole, g_down.whole = lax.optimization_barrier((g_in.left, g_gu.whole, g_down.whole))
    while g_out.step < g_out.steps:
        hop_together(g_out, g_in)
    done = (g_out.left, g_out.right, g_in.left, g_in.right)
    w_out = g_out.result()
    gains = w_out[width:].reshape(extra, n_dp, -1).transpose(1, 0, 2).reshape(n_dp, -1).astype(F32)
    w_out = w_out[:width]
    gain_in = gains[:, :part].reshape(1, model)
    gain_ffn = gains[:, part : 2 * part].reshape(1, model)
    gain_group = gains[:, 2 * part : 2 * part + small].reshape(1, HD)
    h1, _ = norm_forward(seq.astype(F32), gain_in)
    w_in = g_in.result()

    gu1 = g_gu.hop(*done)
    down1 = g_down.hop(*done)
    proj = mm(h1, w_in, NN).astype(BF16)
    y, o, states = rec_forward(proj, seg, gain_group)
    attn_part = after(mm(y, w_out, NN).astype(BF16), *gu1, *down1)
    gu2 = g_gu.hop(attn_part)
    down2 = g_down.hop(attn_part)
    attn = tensor_scatter_sum(attn_part)
    x = tokens.astype(F32)
    x2 = x + g_down.settle(g_gu.settle(after(attn, *gu2, *down2)))
    h2_own, r2 = norm_forward(x2, gain_ffn)
    gu3 = g_gu.hop()
    g_down.store()
    h2 = g_down.settle(g_gu.settle(after(tensor_gather(h2_own), *gu3)))
    gu4 = g_gu.hop()
    down3 = g_down.hop(*gu3)
    w_gu = g_gu.result()
    gu = after(mm(h2, w_gu, NN), *down3)
    down4 = g_down.hop(gu)
    gate, up = gu[:, :hidden_width], gu[:, hidden_width:]
    sg = jax.nn.sigmoid(gate)
    swish = gate * sg
    hidden = (swish * up).astype(BF16)
    d_down_part = after(mm(hidden, cot, TN).astype(BF16), *down4)
    s_down = ring.scatter_sum(d_down_part, 1)
    w_down = g_down.result()
    dh = mm(after(cot, s_down.left, s_down.right), w_down, NT)
    dgate = (dh * up * sg * (1.0 + gate * (1.0 - sg))).astype(BF16)
    dup = (dh * swish).astype(BF16)
    dgu = jnp.concatenate([dgate, dup], axis=1)
    s_down.hop(during=(dgu,))
    d_gu_part = mm(after(h2, s_down.left, s_down.right), dgu, TN).astype(BF16)
    s_down.hop(during=(d_gu_part,))
    s_gu = ring.scatter_sum(d_gu_part, 0)
    dh2_part = mm(after(dgu, s_gu.left, s_gu.right, s_down.left, s_down.right), w_gu, NT).astype(BF16)
    t1 = s_gu.hop(during=(dh2_part,))
    s_down.hop(during=(dh2_part,))
    dh2_part = after(dh2_part, s_down.left, s_down.right)
    dh2 = tensor_scatter_sum(dh2_part)
    step4 = s_down.hop(during=(s_gu.left, s_gu.right))
    s_gu.hop()
    back2, d_gain_ffn = norm_backward(x2, r2, gain_ffn, after(dh2, s_gu.left, s_gu.right, *step4))
    dx2 = cotangent.astype(F32) + back2
    dattn_own = dx2.astype(BF16)
    dattn = tensor_gather(dattn_own)
    d_down = after(s_down.result(), dattn_own)
    ffn_part = mm(after(hidden, dattn_own), w_down, NN).astype(BF16)
    s_gu.hop(during=(ffn_part, d_down))
    dattn = after(dattn, s_gu.left, s_gu.right)
    d_out_part = mm(y, dattn, TN).astype(BF16)
    s_out = ring.scatter_sum(d_out_part, 1)
    ffn = tensor_scatter_sum(after(ffn_part, dattn))
    dy = mm(after(dattn, d_out_part), w_out, NT)
    dproj, d_group = rec_backward(proj, seg, gain_group, o, states, after(dy, s_out.left, s_out.right))
    t4 = s_gu.hop(during=(dproj,))
    s_out.hop(during=(dproj,))
    dh1_part = mm(after(dproj, *t4, s_out.left, s_out.right), w_in, NT).astype(BF16)
    dh1 = tensor_scatter_sum(dh1_part)
    s_out.hop(during=(dh1_part,))
    s_qa = ring.scatter_sum(
        mm(after(h1, dh1_part, s_out.left, s_out.right), dproj[:, : 2 * width], TN).astype(BF16), 0)
    s_out.hop(during=(s_qa.left, s_qa.right))
    s_vz = ring.scatter_sum(
        mm(after(h1, s_qa.left, s_qa.right, s_out.left, s_out.right), dproj[:, 2 * width :], TN).astype(BF16), 0)
    s_qa.hop(during=(s_vz.left, s_vz.right))
    o4 = s_out.hop(during=(s_vz.left, s_vz.right))
    d_gate_up = after(s_gu.result(), s_vz.left, s_vz.right, s_qa.left, s_qa.right, *o4)
    d_gu = d_gate_up.reshape(part, 2, hidden_width)
    s_vz.hop(during=(d_gu,))
    s_qa.hop(during=(d_gu,))
    output = after((x2 + ffn).astype(BF16), s_qa.left, s_qa.right, s_vz.left, s_vz.right)
    r1 = lax.rsqrt(jnp.mean(x * x, axis=-1, keepdims=True) + EPSILON)
    back1, d_gain_in = norm_backward(x, r1, gain_in, after(dh1, output))
    d_gains = jnp.concatenate(
        [d_gain_in.reshape(n_dp, part), d_gain_ffn.reshape(n_dp, part), d_group.reshape(n_dp, small)], axis=1
    )
    d_gains = lax.psum(d_gains, "tensor")
    s_vz.hop(during=(d_gains,))
    s_qa.hop(during=(d_gains,))
    d_tokens = (dx2 + back1).astype(BF16)
    d_gains = scatter_sum_small(after(d_gains, s_qa.left, s_qa.right, s_vz.left, s_vz.right), "dp", n_dp)[0]
    qa4 = s_qa.hop(during=(d_gains, d_tokens))
    s_vz.hop(during=(d_gains, d_tokens))
    d_out = after(s_out.result(), *qa4, s_vz.left, s_vz.right)
    d_qa = s_qa.result().reshape(part, 2, width)
    s_vz.hop(during=(d_qa, d_out))
    d_in = jnp.concatenate([d_qa, s_vz.result().reshape(part, 2, width)], axis=1)
    return (
        output,
        d_tokens,
        d_in,
        d_out,
        d_gu,
        d_down,
        d_gains[:part],
        d_gains[2 * part :],
        d_gains[part : 2 * part],
    )


def solution(mesh):
    split = P("dp", None, "tensor")
    cross = P("tensor", "dp")
    return jax.shard_map(
        functools.partial(body, mesh.shape["dp"], mesh.shape["tensor"]),
        mesh=mesh,
        in_specs=(SPEC_ROWS, P("dp", None), split, cross, split, cross, P("dp"), P("dp"), P("dp"), SPEC_ROWS),
        out_specs=(SPEC_ROWS, SPEC_ROWS, split, cross, split, cross, P("dp"), P("dp"), P("dp")),
        check_vma=False,
    )
```

```python
import functools
import math
import jax
import jax.numpy as jnp
from jax import lax
from jax.experimental import pallas as pl
from jax.experimental.pallas import tpu as pltpu
from jax.sharding import PartitionSpec as P

HD = 128
CHUNK = 128
GROUP_EPSILON = 0.01
F32 = jnp.float32
BF16 = jnp.bfloat16
NN = (((1,), (0,)), ((), ()))
NT = (((1,), (1,)), ((), ()))
TN = (((0,), (0,)), ((), ()))


def mm(a, b, dims):
    return lax.dot_general(a, b, dims, preferred_element_type=F32)


def halves(x):
    high = x.astype(BF16)
    return high, (x - high.astype(F32)).astype(BF16)


def tri_sum(tri, x):
    high, rest = halves(x)
    return mm(tri, high, NN) + mm(tri, rest, NN)


def decays(a_raw, lower):
    sig = jax.nn.sigmoid(a_raw)
    forget = 0.8 + 0.2 * sig
    key = 1.0 - forget
    cum = tri_sum(lower, jnp.log(forget))
    return sig, forget, key, cum


def masks(seg, doc_col, doc_row, block):
    rows = lax.broadcasted_iota(jnp.int32, (CHUNK, CHUNK), 0)
    cols = lax.broadcasted_iota(jnp.int32, (CHUNK, CHUNK), 1)
    causal = rows >= cols
    same = jnp.logical_and(causal, doc_col == doc_row)
    start = block * CHUNK
    end_doc = seg[start + CHUNK - 1]
    last_doc = jnp.where(block > 0, seg[jnp.maximum(start - 1, 0)], -1)
    cont = (doc_col == last_doc).astype(F32)
    tail = (doc_col == end_doc).astype(F32)
    keep = jnp.where(end_doc == last_doc, 1.0, 0.0).astype(F32)
    return causal, same, cont, tail, keep


def forward_kernel(seg, q_ref, a_ref, v_ref, z_ref, col_ref, row_ref, gain_ref,
                   y_ref, o_ref, s_ref, state):
    block = pl.program_id(0)

    @pl.when(block == 0)
    def _():
        state[...] = jnp.zeros_like(state)

    width = q_ref.shape[1]
    causal, same, cont, tail, keep = masks(seg, col_ref[...], row_ref[...], block)
    lower = jnp.where(causal, 1.0, 0.0).astype(BF16)
    _, _, key, cum = decays(a_ref[...].astype(F32), lower)
    total = cum[CHUNK - 1 : CHUNK, :]
    qd, qd_rest = halves(q_ref[...].astype(F32) * jnp.exp(cum))
    kd, kd_rest = halves(key * jnp.exp(-cum))
    kt, kt_rest = halves(key * jnp.exp(total - cum) * tail)
    fade = jnp.exp(total) * keep
    gain = gain_ref[...]
    s_ref[0] = state[...]
    for head in range(width // HD):
        at = slice(head * HD, (head + 1) * HD)
        v = v_ref[:, at]
        st = state[:, at]
        st_high, st_rest = halves(st)
        qh, ql = qd[:, at], qd_rest[:, at]
        scores = mm(qh, kd[:, at], NT) + (mm(qh, kd_rest[:, at], NT) + mm(ql, kd[:, at], NT))
        scores = jnp.where(same, scores, 0.0).astype(BF16)
        earlier = mm(qh, st_high, NT) + (mm(qh, st_rest, NT) + mm(ql, st_high, NT))
        o = mm(scores, v, NN) + cont * earlier
        state[:, at] = st * fade[:, at] + (mm(v, kt[:, at], TN) + mm(v, kt_rest[:, at], TN))
        o_ref[:, at] = o
        z = z_ref[:, at].astype(F32)
        r = lax.rsqrt(jnp.mean(o * o, axis=-1, keepdims=True) + GROUP_EPSILON)
        y_ref[:, at] = (o * r * gain * (z * jax.nn.sigmoid(z))).astype(BF16)


def backward_kernel(seg, q_ref, a_ref, v_ref, z_ref, col_ref, row_ref, gain_ref, o_ref, s_ref, dy_ref,
                    d_ref, dgain_ref, dstate):
    step = pl.program_id(0)
    block = pl.num_programs(0) - 1 - step

    @pl.when(step == 0)
    def _():
        dstate[...] = jnp.zeros_like(dstate)
        dgain_ref[...] = jnp.zeros_like(dgain_ref)

    width = q_ref.shape[1]
    causal, same, cont, tail, keep = masks(seg, col_ref[...], row_ref[...], block)
    lower = jnp.where(causal, 1.0, 0.0).astype(BF16)
    sig, forget, key, cum = decays(a_ref[...].astype(F32), lower)
    total = cum[CHUNK - 1 : CHUNK, :]
    up = jnp.exp(cum)
    down = jnp.exp(-cum)
    late = jnp.exp(total - cum) * tail
    qd = (q_ref[...].astype(F32) * up).astype(BF16)
    kd = (key * down).astype(BF16)
    kt = (key * late).astype(BF16)
    fade = jnp.exp(total) * keep
    gain = gain_ref[...]
    gain_sum = jnp.zeros((1, HD), F32)
    dcums = []
    dkeys = []
    for head in range(width // HD):
        at = slice(head * HD, (head + 1) * HD)
        v = v_ref[:, at]
        o = o_ref[:, at]
        z = z_ref[:, at].astype(F32)
        dy = dy_ref[:, at]
        r = lax.rsqrt(jnp.mean(o * o, axis=-1, keepdims=True) + GROUP_EPSILON)
        n = o * r
        sz = jax.nn.sigmoid(z)
        dng = dy * (z * sz)
        gain_sum += jnp.sum(dng * n, axis=0, keepdims=True)
        dn = dng * gain
        do = (r * (dn - n * jnp.mean(dn * n, axis=-1, keepdims=True))).astype(BF16)
        d_ref[:, 3 * width + head * HD : 3 * width + (head + 1) * HD] = (
            dy * n * gain * (sz * (1.0 + z * (1.0 - sz)))
        ).astype(BF16)
        qh, kh, th = qd[:, at], kd[:, at], kt[:, at]
        scores = jnp.where(same, mm(qh, kh, NT), 0.0).astype(BF16)
        dscores = jnp.where(same, mm(do, v, NT), 0.0).astype(BF16)
        st = s_ref[0, :, at]
        dst = dstate[:, at]
        dst_low = dst.astype(BF16)
        dv = mm(scores, do, TN) + mm(th, dst_low, NT)
        dqd = mm(dscores, kh, NN) + cont * mm(do, st.astype(BF16), NN)
        dkd = mm(dscores, qh, TN)
        dkt = mm(v, dst_low, NN)
        carried = dkt * th.astype(F32)
        dtotal = jnp.sum(carried, axis=0, keepdims=True) + fade[:, at] * jnp.sum(
            dst * st, axis=0, keepdims=True
        )
        dstate[:, at] = dst * fade[:, at] + mm((do.astype(F32) * cont).astype(BF16), qh, TN)
        d_ref[:, head * HD : (head + 1) * HD] = (dqd * up[:, at]).astype(BF16)
        d_ref[:, 2 * width + head * HD : 2 * width + (head + 1) * HD] = dv.astype(BF16)
        dkeys.append(dkd * down[:, at] + dkt * late[:, at])
        dcum = dqd * qh.astype(F32) - dkd * kh.astype(F32) - carried
        high, rest = halves(dcum)
        dlog = mm(lower, high, TN) + mm(lower, rest, TN) + dtotal
        slope = 0.2 * sig[:, at] * (1.0 - sig[:, at])
        d_ref[:, width + head * HD : width + (head + 1) * HD] = (
            (dlog / forget[:, at] - dkeys[-1]) * slope
        ).astype(BF16)
    dgain_ref[...] += gain_sum


def rec_forward(proj, seg, gain):
    length, width = proj.shape[0], proj.shape[1] // 4
    blocks = length // CHUNK
    part = lambda k: pl.BlockSpec((CHUNK, width), lambda i, s, k=k: (i, k))
    return pl.pallas_call(
        forward_kernel,
        grid_spec=pltpu.PrefetchScalarGridSpec(
            num_scalar_prefetch=1,
            grid=(blocks,),
            in_specs=[part(0), part(1), part(2), part(3),
                      pl.BlockSpec((CHUNK, 1), lambda i, s: (i, 0)),
                      pl.BlockSpec((1, CHUNK), lambda i, s: (0, i)),
                      pl.BlockSpec((1, HD), lambda i, s: (0, 0))],
            out_specs=[pl.BlockSpec((CHUNK, width), lambda i, s: (i, 0)),
                       pl.BlockSpec((CHUNK, width), lambda i, s: (i, 0)),
                       pl.BlockSpec((1, HD, width), lambda i, s: (i, 0, 0))],
            scratch_shapes=[pltpu.VMEM((HD, width), F32)],
        ),
        out_shape=[jax.ShapeDtypeStruct((length, width), BF16),
                   jax.ShapeDtypeStruct((length, width), F32),
                   jax.ShapeDtypeStruct((blocks, HD, width), F32)],
        cost_estimate=pl.CostEstimate(flops=30_000_000_000, bytes_accessed=10_000_000, transcendentals=0),
        name="mixer_forward",
    )(seg, proj, proj, proj, proj, seg.reshape(length, 1), seg.reshape(1, length), gain.reshape(1, HD))


def rec_backward(proj, seg, gain, o, states, dy):
    length, width = proj.shape[0], proj.shape[1] // 4
    blocks = length // CHUNK
    last = blocks - 1
    part = lambda k: pl.BlockSpec((CHUNK, width), lambda i, s, k=k: (last - i, k))
    return pl.pallas_call(
        backward_kernel,
        grid_spec=pltpu.PrefetchScalarGridSpec(
            num_scalar_prefetch=1,
            grid=(blocks,),
            in_specs=[part(0), part(1), part(2), part(3),
                      pl.BlockSpec((CHUNK, 1), lambda i, s: (last - i, 0)),
                      pl.BlockSpec((1, CHUNK), lambda i, s: (0, last - i)),
                      pl.BlockSpec((1, HD), lambda i, s: (0, 0)),
                      part(0),
                      pl.BlockSpec((1, HD, width), lambda i, s: (last - i, 0, 0)),
                      part(0)],
            out_specs=[pl.BlockSpec((CHUNK, 4 * width), lambda i, s: (last - i, 0)),
                       pl.BlockSpec((1, HD), lambda i, s: (0, 0))],
            scratch_shapes=[pltpu.VMEM((HD, width), F32)],
        ),
        out_shape=[jax.ShapeDtypeStruct((length, 4 * width), BF16),
                   jax.ShapeDtypeStruct((1, HD), F32)],
        cost_estimate=pl.CostEstimate(flops=60_000_000_000, bytes_accessed=14_000_000, transcendentals=0),
        name="mixer_backward",
    )(seg, proj, proj, proj, proj, seg.reshape(length, 1), seg.reshape(1, length), gain.reshape(1, HD), o, states, dy)


EPSILON = 1e-06
SPEC_ROWS = P(("dp", "tensor"), None)


def ring_order(count):
    return list(range(0, count, 2)) + list(range(count - 1 - count % 2, 0, -2))


class Ring:
    def __init__(self, axis, count):
        order = ring_order(count)
        self.axis, self.count = axis, count
        self.ahead = [(order[i], order[(i + 1) % count]) for i in range(count)]
        self.behind = [(b, a) for a, b in self.ahead]
        self.me = lax.axis_index(axis)
        self.place = jnp.where(self.me % 2 == 0, self.me // 2, count - (self.me + 1) // 2)

    def owner(self, shift):
        at = (self.place + shift + 2 * self.count) % self.count
        return jnp.where(2 * at < self.count, 2 * at, 2 * (self.count - at) - 1)

    def send_ahead(self, x):
        return lax.ppermute(x, self.axis, self.ahead)

    def send_behind(self, x):
        return lax.ppermute(x, self.axis, self.behind)

    def gather(self, x, dim):
        return Gather(self, x, dim)

    def scatter_sum(self, x, dim):
        return ScatterSum(self, x, dim)


def after(x, *earlier):
    return lax.optimization_barrier((x, *earlier))[0]


def first_kernel(at, block, whole):
    whole[...] = block[...]


def pair_kernel(at, left, right, before, whole):
    @pl.when(pl.program_id(0) == 0)
    def _():
        whole[...] = left[...]

    @pl.when(pl.program_id(0) == 1)
    def _():
        whole[...] = right[...]


SMALL_COST = pl.CostEstimate(flops=0, bytes_accessed=4_000_000, transcendentals=0)


class Gather:
    def __init__(self, ring, x, dim, partner=None):
        self.ring, self.dim, self.half = ring, dim, x.shape[0] // 2
        self.column, self.left, self.right = 0, x, x
        self.step, self.steps, self.pending = 0, ring.count // 2, False
        if partner is not None:
            self.box, self.shape, self.column = partner.box, partner.shape, 1
            return
        shape = list(x.shape)
        shape[dim] *= ring.count
        self.shape = jax.ShapeDtypeStruct(tuple(shape), x.dtype)
        self.aligned = x.shape[1] % 128 == 0
        if not self.aligned:
            at = [0, 0]
            at[dim] = ring.me * x.shape[dim]
            self.box = [lax.dynamic_update_slice(jnp.zeros(shape, x.dtype), x, at)]
            return
        to = (lambda i, at: (at[0], 0)) if self.dim == 0 else (lambda i, at: (0, at[0]))
        self.box = [pl.pallas_call(
            first_kernel,
            grid_spec=pltpu.PrefetchScalarGridSpec(
                num_scalar_prefetch=1, grid=(1,), in_specs=[pl.BlockSpec(x.shape, lambda i, at: (0, 0))],
                out_specs=pl.BlockSpec(x.shape, to)),
            out_shape=self.shape, cost_estimate=SMALL_COST, name="gather_first",
        )(self.ring.me.reshape(1), x)]

    @property
    def whole(self):
        return self.box[0]

    @whole.setter
    def whole(self, value):
        self.box[0] = value

    def hop(self, *earlier):
        ring = self.ring
        left, right = self.left, self.right
        if self.step == self.steps:
            return left, right
        step = self.step + 1
        if step == self.steps:
            left, right = left[: self.half], right[self.half :]
        if step > 1:
            left, right, self.whole, *_ = lax.optimization_barrier((left, right, self.whole, *earlier))
        elif earlier:
            left, right, *_ = lax.optimization_barrier((left, right, *earlier))
        left, right = ring.send_ahead(left), ring.send_behind(right)
        if step > 1:
            self.store()
        self.left, self.right, self.step, self.pending = left, right, step, True
        return left, right

    def halves(self):
        if self.step + 1 == self.steps:
            return self.left[: self.half], self.right[self.half :]
        return self.left, self.right

    def send(self, left, right):
        left, right = self.ring.send_ahead(left), self.ring.send_behind(right)
        self.store()
        self.left, self.right, self.step, self.pending = left, right, self.step + 1, True

    def split(self, x, y):
        self.left = self.right = x
        other = Gather(self.ring, y, self.dim, self)
        other.aligned = self.aligned
        return other

    def settle(self, x):
        x, self.whole = lax.optimization_barrier((x, self.whole))
        return x

    def result(self):
        while self.step < self.steps:
            self.hop()
        self.store()
        return self.whole

    def store(self):
        if not self.pending:
            return
        self.pending = False
        ring = self.ring
        last = self.step == self.steps
        if not self.aligned:
            for block, shift in ((self.left, -self.step), (self.right, self.step)):
                at = [self.half if last and shift > 0 else 0, 0]
                at[self.dim] = at[self.dim] + ring.owner(shift) * self.shape.shape[self.dim] // ring.count
                self.whole = lax.dynamic_update_slice(self.whole, block, at)
            return
        owners = jnp.stack([ring.owner(-self.step), ring.owner(self.step)])
        if self.dim == 0 and last:
            to = lambda i, at: (2 * at[i] + i, self.column)
        elif self.dim == 0:
            to = lambda i, at: (at[i], self.column)
        elif last:
            to = lambda i, at: (i, at[i])
        else:
            to = lambda i, at: (0, at[i])
        block = pl.BlockSpec(self.left.shape, lambda i, at: (0, 0))
        self.whole = pl.pallas_call(
            pair_kernel,
            grid_spec=pltpu.PrefetchScalarGridSpec(
                num_scalar_prefetch=1, grid=(2,),
                in_specs=[block, block, pl.BlockSpec(memory_space=pl.ANY)],
                out_specs=pl.BlockSpec(self.left.shape, to)),
            out_shape=self.shape, input_output_aliases={3: 0}, cost_estimate=SMALL_COST, name="gather_pair",
        )(owners, self.left, self.right, self.whole)


def hop_together(one, two):
    if one.step == one.steps:
        return
    blocks = *one.halves(), *two.halves()
    if one.step:
        *blocks, one.whole, two.whole = lax.optimization_barrier((*blocks, one.whole, two.whole))
    one.send(*blocks[:2])
    two.send(*blocks[2:])


def finish_kernel(parts, at, left, right, own, total):
    both = left[...].astype(F32) + right[...].astype(F32) + own[...].astype(F32)
    width = both.shape[1] // parts
    for k in range(parts):
        total[:, k, :] = both[:, k * width : (k + 1) * width]


class ScatterSum:
    def __init__(self, ring, x, dim):
        self.ring, self.dim, self.x = ring, dim, x
        shape = list(x.shape)
        shape[dim] //= ring.count
        self.size, self.half = shape[dim], shape[0] // 2
        self.shape, self.step, self.steps = shape, 0, ring.count // 2
        self.left = self.part(self.steps)[: self.half]
        self.right = self.part(-self.steps)[self.half :]

    def part(self, shift):
        at = [0, 0]
        at[self.dim] = self.ring.owner(shift) * self.size
        return lax.dynamic_slice(self.x, at, self.shape)

    def hop(self, before=(), during=()):
        ring, left, right = self.ring, self.left, self.right
        if self.step == self.steps:
            return self.arrived
        self.step += 1
        left, right, *_ = lax.optimization_barrier((left, right, *before))
        left, right = ring.send_ahead(left), ring.send_behind(right)
        left, right, *_ = lax.optimization_barrier((left, right, *during))
        self.arrived = left, right
        shift = self.steps - self.step
        if self.step == 1:
            ahead, behind = self.part(shift), self.part(-shift)
            rest, zero = ahead.shape[0] - self.half, jnp.zeros((), left.dtype)
            self.left = lax.pad(left, zero, ((0, rest, 0), (0, 0, 0))) + ahead
            self.right = lax.pad(right, zero, ((self.half, 0, 0), (0, 0, 0))) + behind
        elif shift:
            self.left, self.right = left + self.part(shift), right + self.part(-shift)
        return self.arrived

    def finish(self, parts):
        while self.step < self.steps:
            self.hop()
        left, right = self.arrived
        rows, columns = left.shape
        tile = min(64, rows)
        near = pl.BlockSpec((tile, columns), lambda i, at: (i, 0))
        mine = pl.BlockSpec((tile, columns), lambda i, at: (at[0] * (rows // tile) + i, 0))
        return pl.pallas_call(
            functools.partial(finish_kernel, parts),
            grid_spec=pltpu.PrefetchScalarGridSpec(
                num_scalar_prefetch=1, grid=(rows // tile,), in_specs=[near, near, mine],
                out_specs=pl.BlockSpec((tile, parts, columns // parts), lambda i, at: (i, 0, 0))),
            out_shape=jax.ShapeDtypeStruct((rows, parts, columns // parts), F32),
            cost_estimate=SMALL_COST, name="finish",
        )(self.ring.me.reshape(1), left, right, self.x)

    def result(self):
        while self.step < self.steps:
            self.hop()
        left, right = self.arrived
        return left.astype(F32) + right.astype(F32) + self.part(0).astype(F32)


def gather_small(row, axis, count):
    me = lax.axis_index(axis)
    whole = lax.dynamic_update_slice(jnp.zeros((count, row.shape[1]), row.dtype), row, (me, 0))
    for turn in range(1, count):
        got = lax.ppermute(row, axis, [(i, (i + turn) % count) for i in range(count)])
        whole = lax.dynamic_update_slice(whole, got, ((me - turn + count) % count, 0))
    return whole


def scatter_sum_small(rows, axis, count):
    me = lax.axis_index(axis)
    if count & (count - 1):
        return lax.dynamic_slice_in_dim(lax.psum(rows, axis), me, 1, 0)
    while count > 1:
        count //= 2
        side = me // count % 2
        mine = lax.dynamic_slice_in_dim(rows, side * count, count, 0)
        other = lax.dynamic_slice_in_dim(rows, (1 - side) * count, count, 0)
        whole = lax.axis_size(axis)
        rows = mine + lax.ppermute(other, axis, [(i, i ^ count) for i in range(whole)])
    return rows


def norm_forward(values, gain):
    r = lax.rsqrt(jnp.mean(values * values, axis=-1, keepdims=True) + EPSILON)
    return (values * r * gain).astype(BF16), r


def norm_backward(values, r, gain, grad):
    n = values * r
    scaled = grad * gain
    back = r * (scaled - n * jnp.mean(scaled * n, axis=-1, keepdims=True))
    return back, jnp.sum(grad * n, axis=0)


def tensor_gather(x):
    return lax.all_gather(x, "tensor", axis=0, tiled=True)


def tensor_scatter_sum(x):
    return lax.psum_scatter(x, "tensor", scatter_dimension=0, tiled=True).astype(F32)


def body(n_dp, n_tensor, tokens, segment_ids, mixer_in, mixer_out, gate_up, down,
         norm_gain, group_gain, ffn_gain, cotangent):
    ring = Ring("dp", n_dp)
    seg = segment_ids[0]
    part, small = norm_gain.shape[0], group_gain.shape[0]
    model = part * n_dp
    width = mixer_out.shape[0]
    hidden_width = down.shape[0]

    in_part = mixer_in.reshape(part, 4 * width)
    gu_part = gate_up.reshape(part, 2 * hidden_width)
    extra = 32
    gain_rows = jnp.concatenate([norm_gain, ffn_gain, group_gain])
    gain_rows = jnp.pad(gain_rows, (0, extra * mixer_out.shape[1] - gain_rows.shape[0]))
    out_part = jnp.concatenate([mixer_out, gain_rows.reshape(extra, mixer_out.shape[1])], axis=0)
    seq = tensor_gather(tokens)
    cot = tensor_gather(cotangent)

    g_in, g_out = ring.gather(in_part, 0), ring.gather(out_part, 1)
    hop_together(g_out, g_in)
    g_gu, g_down = ring.gather(gu_part, 0), ring.gather(down, 1)
    g_up = g_gu.split(gu_part[:, :hidden_width], gu_part[:, hidden_width:])
    hop_together(g_out, g_in)
    g_in.left, g_gu.whole, g_down.whole = lax.optimization_barrier((g_in.left, g_gu.whole, g_down.whole))
    while g_out.step < g_out.steps:
        hop_together(g_out, g_in)
    done = (g_out.left, g_out.right, g_in.left, g_in.right)
    w_out = g_out.result()
    gains = w_out[width:].reshape(extra, n_dp, -1).transpose(1, 0, 2).reshape(n_dp, -1).astype(F32)
    w_out = w_out[:width]
    gain_in = gains[:, :part].reshape(1, model)
    gain_ffn = gains[:, part : 2 * part].reshape(1, model)
    gain_group = gains[:, 2 * part : 2 * part + small].reshape(1, HD)
    h1, _ = norm_forward(seq.astype(F32), gain_in)
    w_in = g_in.result()

    gate1 = g_gu.hop(*done)
    up1 = g_up.hop(*done)
    down1 = g_down.hop(*done)
    proj = mm(h1, w_in, NN).astype(BF16)
    y, o, states = rec_forward(proj, seg, gain_group)
    attn_part = after(mm(y, w_out, NN).astype(BF16), *gate1, *up1, *down1)
    g_gu.hop(attn_part)
    g_up.hop(attn_part)
    attn = tensor_scatter_sum(attn_part)
    x = tokens.astype(F32)
    gate3 = g_gu.hop()
    g_down.store()
    x2 = x + g_down.settle(g_gu.settle(after(attn, *gate3, g_up.left, g_up.right)))
    h2_own, r2 = norm_forward(x2, gain_ffn)
    g_up.hop()
    g_gu.hop()
    g_up.hop()
    h2 = g_gu.settle(after(tensor_gather(h2_own), g_gu.left, g_gu.right, g_up.left, g_up.right))
    down2 = g_down.hop(g_up.left, g_up.right)
    g_gu.store()
    w_gu = g_up.result()
    gu = after(mm(h2, w_gu, NN), *down2)
    down3 = g_down.hop(gu)
    gate, up = gu[:, :hidden_width], gu[:, hidden_width:]
    sg = jax.nn.sigmoid(gate)
    swish = gate * sg
    hidden = (swish * up).astype(BF16)
    d_down_part = after(mm(hidden, cot, TN).astype(BF16), *down3)
    down4 = g_down.hop(d_down_part)
    s_down = ring.scatter_sum(d_down_part, 1)
    step1 = s_down.hop()
    w_down = g_down.result()
    dh = mm(after(cot, s_down.left, s_down.right), w_down, NT)
    dgate = (dh * up * sg * (1.0 + gate * (1.0 - sg))).astype(BF16)
    dup = (dh * swish).astype(BF16)
    dgu = jnp.concatenate([dgate, dup], axis=1)
    s_down.hop(during=(dgu,))
    d_gu_part = mm(after(h2, s_down.left, s_down.right), dgu, TN).astype(BF16)
    s_down.hop(during=(d_gu_part,))
    s_gu = ring.scatter_sum(d_gu_part, 0)
    dh2_part = mm(after(dgu, s_gu.left, s_gu.right, s_down.left, s_down.right), w_gu, NT).astype(BF16)
    t1 = s_gu.hop(during=(dh2_part,))
    dh2_part = after(dh2_part, *t1)
    dh2 = tensor_scatter_sum(dh2_part)
    s_gu.hop()
    back2, d_gain_ffn = norm_backward(x2, r2, gain_ffn, after(dh2, s_gu.left, s_gu.right))
    dx2 = cotangent.astype(F32) + back2
    dattn_own = dx2.astype(BF16)
    dattn = tensor_gather(dattn_own)
    ffn_part = mm(after(hidden, dattn_own), w_down, NN).astype(BF16)
    s_gu.hop(during=(ffn_part,))
    dattn = after(dattn, s_gu.left, s_gu.right)
    d_out_part = mm(y, dattn, TN).astype(BF16)
    s_out = ring.scatter_sum(d_out_part, 1)
    ffn = tensor_scatter_sum(after(ffn_part, dattn))
    dy = mm(after(dattn, d_out_part), w_out, NT)
    dproj, d_group = rec_backward(proj, seg, gain_group, o, states, dy)
    t4 = s_gu.hop(during=(dproj,))
    dh1_part = mm(after(dproj, *t4), w_in, NT).astype(BF16)
    dh1 = tensor_scatter_sum(dh1_part)
    step4 = s_down.hop(before=(dproj,), during=(dh1_part,))
    s_out.hop(before=(dproj,), during=(dh1_part,))
    s_in = ring.scatter_sum(mm(after(h1, dh1_part), dproj, TN).astype(BF16), 0)
    o2 = s_out.hop(before=(s_in.left, s_in.right))
    s_in.hop(before=step4)
    r1 = lax.rsqrt(jnp.mean(x * x, axis=-1, keepdims=True) + EPSILON)
    back1, d_gain_in = norm_backward(x, r1, gain_in, after(dh1, s_in.left, s_in.right))
    d_gains = jnp.concatenate(
        [d_gain_in.reshape(n_dp, part), d_gain_ffn.reshape(n_dp, part), d_group.reshape(n_dp, small)], axis=1
    )
    d_gains = lax.psum(d_gains, "tensor")
    s_in.hop(before=o2, during=(d_gains,))
    o3 = s_out.hop()
    d_tokens = after((dx2 + back1).astype(BF16), s_in.left, s_in.right)
    d_gains = scatter_sum_small(after(d_gains, s_in.left, s_in.right), "dp", n_dp)[0]
    s_in.hop(before=o3, during=(d_tokens,))
    o4 = s_out.hop()
    d_gu = after(s_gu.arrived[0], s_in.left, s_in.right)
    s_gu.arrived = d_gu, s_gu.arrived[1]
    d_gu = s_gu.finish(2)
    d_down = after(s_down.result(), s_in.left, s_in.right)
    d_out = after(s_out.result(), s_in.left, s_in.right)
    output = (x2 + after(ffn, s_in.left, s_in.right)).astype(BF16)
    s_in.hop(before=o4, during=(d_gu, d_down, d_out, output))
    d_in = s_in.finish(4)
    return (
        output,
        d_tokens,
        d_in,
        d_out,
        d_gu,
        d_down,
        d_gains[:part],
        d_gains[2 * part :],
        d_gains[part : 2 * part],
    )


def solution(mesh):
    split = P("dp", None, "tensor")
    cross = P("tensor", "dp")
    return jax.shard_map(
        functools.partial(body, mesh.shape["dp"], mesh.shape["tensor"]),
        mesh=mesh,
        in_specs=(SPEC_ROWS, P("dp", None), split, cross, split, cross, P("dp"), P("dp"), P("dp"), SPEC_ROWS),
        out_specs=(SPEC_ROWS, SPEC_ROWS, split, cross, split, cross, P("dp"), P("dp"), P("dp")),
        check_vma=False,
    )
```

```python
import functools
import math
import jax
import jax.numpy as jnp
from jax import lax
from jax.experimental import pallas as pl
from jax.experimental.pallas import tpu as pltpu
from jax.sharding import PartitionSpec as P

HD = 128
CHUNK = 128
GROUP_EPSILON = 0.01
F32 = jnp.float32
BF16 = jnp.bfloat16
NN = (((1,), (0,)), ((), ()))
NT = (((1,), (1,)), ((), ()))
TN = (((0,), (0,)), ((), ()))


def mm(a, b, dims):
    return lax.dot_general(a, b, dims, preferred_element_type=F32)


def halves(x):
    high = x.astype(BF16)
    return high, (x - high.astype(F32)).astype(BF16)


def tri_sum(tri, x):
    high, rest = halves(x)
    return mm(tri, high, NN) + mm(tri, rest, NN)


def decays(a_raw, lower):
    sig = jax.nn.sigmoid(a_raw)
    forget = 0.8 + 0.2 * sig
    key = 1.0 - forget
    cum = tri_sum(lower, jnp.log(forget))
    return sig, forget, key, cum


def masks(seg, doc_col, doc_row, block):
    rows = lax.broadcasted_iota(jnp.int32, (CHUNK, CHUNK), 0)
    cols = lax.broadcasted_iota(jnp.int32, (CHUNK, CHUNK), 1)
    causal = rows >= cols
    same = jnp.logical_and(causal, doc_col == doc_row)
    start = block * CHUNK
    end_doc = seg[start + CHUNK - 1]
    last_doc = jnp.where(block > 0, seg[jnp.maximum(start - 1, 0)], -1)
    cont = (doc_col == last_doc).astype(F32)
    tail = (doc_col == end_doc).astype(F32)
    keep = jnp.where(end_doc == last_doc, 1.0, 0.0).astype(F32)
    return causal, same, cont, tail, keep


def forward_kernel(seg, q_ref, a_ref, v_ref, z_ref, col_ref, row_ref, gain_ref,
                   y_ref, o_ref, s_ref, state):
    block = pl.program_id(0)

    @pl.when(block == 0)
    def _():
        state[...] = jnp.zeros_like(state)

    width = q_ref.shape[1]
    causal, same, cont, tail, keep = masks(seg, col_ref[...], row_ref[...], block)
    lower = jnp.where(causal, 1.0, 0.0).astype(BF16)
    _, _, key, cum = decays(a_ref[...].astype(F32), lower)
    total = cum[CHUNK - 1 : CHUNK, :]
    qd, qd_rest = halves(q_ref[...].astype(F32) * jnp.exp(cum))
    kd, kd_rest = halves(key * jnp.exp(-cum))
    kt, kt_rest = halves(key * jnp.exp(total - cum) * tail)
    fade = jnp.exp(total) * keep
    gain = gain_ref[...]
    s_ref[0] = state[...]
    for head in range(width // HD):
        at = slice(head * HD, (head + 1) * HD)
        v = v_ref[:, at]
        st = state[:, at]
        st_high, st_rest = halves(st)
        qh, ql = qd[:, at], qd_rest[:, at]
        scores = mm(qh, kd[:, at], NT) + (mm(qh, kd_rest[:, at], NT) + mm(ql, kd[:, at], NT))
        scores = jnp.where(same, scores, 0.0).astype(BF16)
        earlier = mm(qh, st_high, NT) + (mm(qh, st_rest, NT) + mm(ql, st_high, NT))
        o = mm(scores, v, NN) + cont * earlier
        state[:, at] = st * fade[:, at] + (mm(v, kt[:, at], TN) + mm(v, kt_rest[:, at], TN))
        o_ref[:, at] = o
        z = z_ref[:, at].astype(F32)
        r = lax.rsqrt(jnp.mean(o * o, axis=-1, keepdims=True) + GROUP_EPSILON)
        y_ref[:, at] = (o * r * gain * (z * jax.nn.sigmoid(z))).astype(BF16)


def backward_kernel(seg, q_ref, a_ref, v_ref, z_ref, col_ref, row_ref, gain_ref, o_ref, s_ref, dy_ref,
                    d_ref, dgain_ref, dstate):
    step = pl.program_id(0)
    block = pl.num_programs(0) - 1 - step

    @pl.when(step == 0)
    def _():
        dstate[...] = jnp.zeros_like(dstate)
        dgain_ref[...] = jnp.zeros_like(dgain_ref)

    width = q_ref.shape[1]
    causal, same, cont, tail, keep = masks(seg, col_ref[...], row_ref[...], block)
    lower = jnp.where(causal, 1.0, 0.0).astype(BF16)
    sig, forget, key, cum = decays(a_ref[...].astype(F32), lower)
    total = cum[CHUNK - 1 : CHUNK, :]
    up = jnp.exp(cum)
    down = jnp.exp(-cum)
    late = jnp.exp(total - cum) * tail
    qd = (q_ref[...].astype(F32) * up).astype(BF16)
    kd = (key * down).astype(BF16)
    kt = (key * late).astype(BF16)
    fade = jnp.exp(total) * keep
    gain = gain_ref[...]
    gain_sum = jnp.zeros((1, HD), F32)
    dcums = []
    dkeys = []
    for head in range(width // HD):
        at = slice(head * HD, (head + 1) * HD)
        v = v_ref[:, at]
        o = o_ref[:, at]
        z = z_ref[:, at].astype(F32)
        dy = dy_ref[:, at]
        r = lax.rsqrt(jnp.mean(o * o, axis=-1, keepdims=True) + GROUP_EPSILON)
        n = o * r
        sz = jax.nn.sigmoid(z)
        dng = dy * (z * sz)
        gain_sum += jnp.sum(dng * n, axis=0, keepdims=True)
        dn = dng * gain
        do = (r * (dn - n * jnp.mean(dn * n, axis=-1, keepdims=True))).astype(BF16)
        d_ref[:, 3 * width + head * HD : 3 * width + (head + 1) * HD] = (
            dy * n * gain * (sz * (1.0 + z * (1.0 - sz)))
        ).astype(BF16)
        qh, kh, th = qd[:, at], kd[:, at], kt[:, at]
        scores = jnp.where(same, mm(qh, kh, NT), 0.0).astype(BF16)
        dscores = jnp.where(same, mm(do, v, NT), 0.0).astype(BF16)
        st = s_ref[0, :, at]
        dst = dstate[:, at]
        dst_low = dst.astype(BF16)
        dv = mm(scores, do, TN) + mm(th, dst_low, NT)
        dqd = mm(dscores, kh, NN) + cont * mm(do, st.astype(BF16), NN)
        dkd = mm(dscores, qh, TN)
        dkt = mm(v, dst_low, NN)
        carried = dkt * th.astype(F32)
        dtotal = jnp.sum(carried, axis=0, keepdims=True) + fade[:, at] * jnp.sum(
            dst * st, axis=0, keepdims=True
        )
        dstate[:, at] = dst * fade[:, at] + mm((do.astype(F32) * cont).astype(BF16), qh, TN)
        d_ref[:, head * HD : (head + 1) * HD] = (dqd * up[:, at]).astype(BF16)
        d_ref[:, 2 * width + head * HD : 2 * width + (head + 1) * HD] = dv.astype(BF16)
        dkeys.append(dkd * down[:, at] + dkt * late[:, at])
        dcum = dqd * qh.astype(F32) - dkd * kh.astype(F32) - carried
        high, rest = halves(dcum)
        dlog = mm(lower, high, TN) + mm(lower, rest, TN) + dtotal
        slope = 0.2 * sig[:, at] * (1.0 - sig[:, at])
        d_ref[:, width + head * HD : width + (head + 1) * HD] = (
            (dlog / forget[:, at] - dkeys[-1]) * slope
        ).astype(BF16)
    dgain_ref[...] += gain_sum


def rec_forward(proj, seg, gain):
    length, width = proj.shape[0], proj.shape[1] // 4
    blocks = length // CHUNK
    part = lambda k: pl.BlockSpec((CHUNK, width), lambda i, s, k=k: (i, k))
    return pl.pallas_call(
        forward_kernel,
        grid_spec=pltpu.PrefetchScalarGridSpec(
            num_scalar_prefetch=1,
            grid=(blocks,),
            in_specs=[part(0), part(1), part(2), part(3),
                      pl.BlockSpec((CHUNK, 1), lambda i, s: (i, 0)),
                      pl.BlockSpec((1, CHUNK), lambda i, s: (0, i)),
                      pl.BlockSpec((1, HD), lambda i, s: (0, 0))],
            out_specs=[pl.BlockSpec((CHUNK, width), lambda i, s: (i, 0)),
                       pl.BlockSpec((CHUNK, width), lambda i, s: (i, 0)),
                       pl.BlockSpec((1, HD, width), lambda i, s: (i, 0, 0))],
            scratch_shapes=[pltpu.VMEM((HD, width), F32)],
        ),
        out_shape=[jax.ShapeDtypeStruct((length, width), BF16),
                   jax.ShapeDtypeStruct((length, width), F32),
                   jax.ShapeDtypeStruct((blocks, HD, width), F32)],
        cost_estimate=pl.CostEstimate(flops=30_000_000_000, bytes_accessed=10_000_000, transcendentals=0),
        name="mixer_forward",
    )(seg, proj, proj, proj, proj, seg.reshape(length, 1), seg.reshape(1, length), gain.reshape(1, HD))


def rec_backward(proj, seg, gain, o, states, dy):
    length, width = proj.shape[0], proj.shape[1] // 4
    blocks = length // CHUNK
    last = blocks - 1
    part = lambda k: pl.BlockSpec((CHUNK, width), lambda i, s, k=k: (last - i, k))
    return pl.pallas_call(
        backward_kernel,
        grid_spec=pltpu.PrefetchScalarGridSpec(
            num_scalar_prefetch=1,
            grid=(blocks,),
            in_specs=[part(0), part(1), part(2), part(3),
                      pl.BlockSpec((CHUNK, 1), lambda i, s: (last - i, 0)),
                      pl.BlockSpec((1, CHUNK), lambda i, s: (0, last - i)),
                      pl.BlockSpec((1, HD), lambda i, s: (0, 0)),
                      part(0),
                      pl.BlockSpec((1, HD, width), lambda i, s: (last - i, 0, 0)),
                      part(0)],
            out_specs=[pl.BlockSpec((CHUNK, 4 * width), lambda i, s: (last - i, 0)),
                       pl.BlockSpec((1, HD), lambda i, s: (0, 0))],
            scratch_shapes=[pltpu.VMEM((HD, width), F32)],
        ),
        out_shape=[jax.ShapeDtypeStruct((length, 4 * width), BF16),
                   jax.ShapeDtypeStruct((1, HD), F32)],
        cost_estimate=pl.CostEstimate(flops=60_000_000_000, bytes_accessed=14_000_000, transcendentals=0),
        name="mixer_backward",
    )(seg, proj, proj, proj, proj, seg.reshape(length, 1), seg.reshape(1, length), gain.reshape(1, HD), o, states, dy)


EPSILON = 1e-06
SPEC_ROWS = P(("dp", "tensor"), None)


def ring_order(count):
    return list(range(0, count, 2)) + list(range(count - 1 - count % 2, 0, -2))


class Ring:
    def __init__(self, axis, count):
        order = ring_order(count)
        self.axis, self.count = axis, count
        self.ahead = [(order[i], order[(i + 1) % count]) for i in range(count)]
        self.behind = [(b, a) for a, b in self.ahead]
        self.me = lax.axis_index(axis)
        self.place = jnp.where(self.me % 2 == 0, self.me // 2, count - (self.me + 1) // 2)

    def owner(self, shift):
        at = (self.place + shift + 2 * self.count) % self.count
        return jnp.where(2 * at < self.count, 2 * at, 2 * (self.count - at) - 1)

    def send_ahead(self, x):
        return lax.ppermute(x, self.axis, self.ahead)

    def send_behind(self, x):
        return lax.ppermute(x, self.axis, self.behind)

    def gather(self, x, dim):
        return Gather(self, x, dim)

    def scatter_sum(self, x, dim):
        return ScatterSum(self, x, dim)


def after(x, *earlier):
    return lax.optimization_barrier((x, *earlier))[0]


def first_kernel(at, block, whole):
    whole[...] = block[...]


def pair_kernel(at, left, right, before, whole):
    @pl.when(pl.program_id(0) == 0)
    def _():
        whole[...] = left[...]

    @pl.when(pl.program_id(0) == 1)
    def _():
        whole[...] = right[...]


SMALL_COST = pl.CostEstimate(flops=0, bytes_accessed=4_000_000, transcendentals=0)


class Gather:
    def __init__(self, ring, x, dim, partner=None):
        self.ring, self.dim, self.half = ring, dim, x.shape[0] // 2
        self.column, self.left, self.right = 0, x, x
        self.step, self.steps, self.pending = 0, ring.count // 2, False
        if partner is not None:
            self.box, self.shape, self.column = partner.box, partner.shape, 1
            return
        shape = list(x.shape)
        shape[dim] *= ring.count
        self.shape = jax.ShapeDtypeStruct(tuple(shape), x.dtype)
        self.aligned = x.shape[1] % 128 == 0
        if not self.aligned:
            at = [0, 0]
            at[dim] = ring.me * x.shape[dim]
            self.box = [lax.dynamic_update_slice(jnp.zeros(shape, x.dtype), x, at)]
            return
        to = (lambda i, at: (at[0], 0)) if self.dim == 0 else (lambda i, at: (0, at[0]))
        self.box = [pl.pallas_call(
            first_kernel,
            grid_spec=pltpu.PrefetchScalarGridSpec(
                num_scalar_prefetch=1, grid=(1,), in_specs=[pl.BlockSpec(x.shape, lambda i, at: (0, 0))],
                out_specs=pl.BlockSpec(x.shape, to)),
            out_shape=self.shape, cost_estimate=SMALL_COST, name="gather_first",
        )(self.ring.me.reshape(1), x)]

    @property
    def whole(self):
        return self.box[0]

    @whole.setter
    def whole(self, value):
        self.box[0] = value

    def hop(self, *earlier):
        ring = self.ring
        left, right = self.left, self.right
        if self.step == self.steps:
            return left, right
        step = self.step + 1
        if step == self.steps:
            left, right = left[: self.half], right[self.half :]
        if step > 1:
            left, right, self.whole, *_ = lax.optimization_barrier((left, right, self.whole, *earlier))
        elif earlier:
            left, right, *_ = lax.optimization_barrier((left, right, *earlier))
        left, right = ring.send_ahead(left), ring.send_behind(right)
        if step > 1:
            self.store()
        self.left, self.right, self.step, self.pending = left, right, step, True
        return left, right

    def halves(self):
        if self.step + 1 == self.steps:
            return self.left[: self.half], self.right[self.half :]
        return self.left, self.right

    def send(self, left, right):
        left, right = self.ring.send_ahead(left), self.ring.send_behind(right)
        self.store()
        self.left, self.right, self.step, self.pending = left, right, self.step + 1, True

    def split(self, x, y):
        self.left = self.right = x
        other = Gather(self.ring, y, self.dim, self)
        other.aligned = self.aligned
        return other

    def settle(self, x):
        x, self.whole = lax.optimization_barrier((x, self.whole))
        return x

    def result(self):
        while self.step < self.steps:
            self.hop()
        self.store()
        return self.whole

    def store(self):
        if not self.pending:
            return
        self.pending = False
        ring = self.ring
        last = self.step == self.steps
        if not self.aligned:
            for block, shift in ((self.left, -self.step), (self.right, self.step)):
                at = [self.half if last and shift > 0 else 0, 0]
                at[self.dim] = at[self.dim] + ring.owner(shift) * self.shape.shape[self.dim] // ring.count
                self.whole = lax.dynamic_update_slice(self.whole, block, at)
            return
        owners = jnp.stack([ring.owner(-self.step), ring.owner(self.step)])
        if self.dim == 0 and last:
            to = lambda i, at: (2 * at[i] + i, self.column)
        elif self.dim == 0:
            to = lambda i, at: (at[i], self.column)
        elif last:
            to = lambda i, at: (i, at[i])
        else:
            to = lambda i, at: (0, at[i])
        block = pl.BlockSpec(self.left.shape, lambda i, at: (0, 0))
        self.whole = pl.pallas_call(
            pair_kernel,
            grid_spec=pltpu.PrefetchScalarGridSpec(
                num_scalar_prefetch=1, grid=(2,),
                in_specs=[block, block, pl.BlockSpec(memory_space=pl.ANY)],
                out_specs=pl.BlockSpec(self.left.shape, to)),
            out_shape=self.shape, input_output_aliases={3: 0}, cost_estimate=SMALL_COST, name="gather_pair",
        )(owners, self.left, self.right, self.whole)


def hop_together(one, two):
    if one.step == one.steps:
        return
    blocks = *one.halves(), *two.halves()
    if one.step:
        *blocks, one.whole, two.whole = lax.optimization_barrier((*blocks, one.whole, two.whole))
    one.send(*blocks[:2])
    two.send(*blocks[2:])


def finish_kernel(parts, at, left, right, own, total):
    both = left[...].astype(F32) + right[...].astype(F32) + own[...].astype(F32)
    width = both.shape[1] // parts
    for k in range(parts):
        total[:, k, :] = both[:, k * width : (k + 1) * width]


class ScatterSum:
    def __init__(self, ring, x, dim):
        self.ring, self.dim, self.x = ring, dim, x
        shape = list(x.shape)
        shape[dim] //= ring.count
        self.size, self.half = shape[dim], shape[0] // 2
        self.shape, self.step, self.steps = shape, 0, ring.count // 2
        self.left = self.part(self.steps)[: self.half]
        self.right = self.part(-self.steps)[self.half :]

    def part(self, shift):
        at = [0, 0]
        at[self.dim] = self.ring.owner(shift) * self.size
        return lax.dynamic_slice(self.x, at, self.shape)

    def hop(self, before=(), during=()):
        ring, left, right = self.ring, self.left, self.right
        if self.step == self.steps:
            return self.arrived
        self.step += 1
        left, right, *_ = lax.optimization_barrier((left, right, *before))
        left, right = ring.send_ahead(left), ring.send_behind(right)
        left, right, *_ = lax.optimization_barrier((left, right, *during))
        self.arrived = left, right
        shift = self.steps - self.step
        if self.step == 1:
            ahead, behind = self.part(shift), self.part(-shift)
            rest, zero = ahead.shape[0] - self.half, jnp.zeros((), left.dtype)
            self.left = lax.pad(left, zero, ((0, rest, 0), (0, 0, 0))) + ahead
            self.right = lax.pad(right, zero, ((self.half, 0, 0), (0, 0, 0))) + behind
        elif shift:
            self.left, self.right = left + self.part(shift), right + self.part(-shift)
        return self.arrived

    def finish(self, parts):
        while self.step < self.steps:
            self.hop()
        left, right = self.arrived
        rows, columns = left.shape
        tile = min(64, rows)
        near = pl.BlockSpec((tile, columns), lambda i, at: (i, 0))
        mine = pl.BlockSpec((tile, columns), lambda i, at: (at[0] * (rows // tile) + i, 0))
        return pl.pallas_call(
            functools.partial(finish_kernel, parts),
            grid_spec=pltpu.PrefetchScalarGridSpec(
                num_scalar_prefetch=1, grid=(rows // tile,), in_specs=[near, near, mine],
                out_specs=pl.BlockSpec((tile, parts, columns // parts), lambda i, at: (i, 0, 0))),
            out_shape=jax.ShapeDtypeStruct((rows, parts, columns // parts), F32),
            cost_estimate=SMALL_COST, name="finish",
        )(self.ring.me.reshape(1), left, right, self.x)

    def result(self):
        while self.step < self.steps:
            self.hop()
        left, right = self.arrived
        return left.astype(F32) + right.astype(F32) + self.part(0).astype(F32)


def gather_small(row, axis, count):
    me = lax.axis_index(axis)
    whole = lax.dynamic_update_slice(jnp.zeros((count, row.shape[1]), row.dtype), row, (me, 0))
    for turn in range(1, count):
        got = lax.ppermute(row, axis, [(i, (i + turn) % count) for i in range(count)])
        whole = lax.dynamic_update_slice(whole, got, ((me - turn + count) % count, 0))
    return whole


def scatter_sum_small(rows, axis, count):
    me = lax.axis_index(axis)
    if count & (count - 1):
        return lax.dynamic_slice_in_dim(lax.psum(rows, axis), me, 1, 0)
    while count > 1:
        count //= 2
        side = me // count % 2
        mine = lax.dynamic_slice_in_dim(rows, side * count, count, 0)
        other = lax.dynamic_slice_in_dim(rows, (1 - side) * count, count, 0)
        whole = lax.axis_size(axis)
        rows = mine + lax.ppermute(other, axis, [(i, i ^ count) for i in range(whole)])
    return rows


def norm_forward(values, gain):
    r = lax.rsqrt(jnp.mean(values * values, axis=-1, keepdims=True) + EPSILON)
    return (values * r * gain).astype(BF16), r


def norm_backward(values, r, gain, grad):
    n = values * r
    scaled = grad * gain
    back = r * (scaled - n * jnp.mean(scaled * n, axis=-1, keepdims=True))
    return back, jnp.sum(grad * n, axis=0)


def tensor_gather(x):
    return lax.all_gather(x, "tensor", axis=0, tiled=True)


def tensor_scatter_sum(x):
    return lax.psum_scatter(x, "tensor", scatter_dimension=0, tiled=True).astype(F32)


def body(n_dp, n_tensor, tokens, segment_ids, mixer_in, mixer_out, gate_up, down,
         norm_gain, group_gain, ffn_gain, cotangent):
    ring = Ring("dp", n_dp)
    seg = segment_ids[0]
    part, small = norm_gain.shape[0], group_gain.shape[0]
    model = part * n_dp
    width = mixer_out.shape[0]
    hidden_width = down.shape[0]

    in_part = mixer_in.reshape(part, 4 * width)
    gu_part = gate_up.reshape(part, 2 * hidden_width)
    extra = 32
    gain_rows = jnp.concatenate([norm_gain, ffn_gain, group_gain])
    gain_rows = jnp.pad(gain_rows, (0, extra * mixer_out.shape[1] - gain_rows.shape[0]))
    out_part = jnp.concatenate([mixer_out, gain_rows.reshape(extra, mixer_out.shape[1])], axis=0)
    seq = tensor_gather(tokens)
    cot = tensor_gather(cotangent)

    g_in, g_out = ring.gather(in_part, 0), ring.gather(out_part, 1)
    hop_together(g_out, g_in)
    g_gu, g_down = ring.gather(gu_part, 0), ring.gather(down, 1)
    g_up = g_gu.split(gu_part[:, :hidden_width], gu_part[:, hidden_width:])
    hop_together(g_out, g_in)
    g_in.left, g_gu.whole, g_down.whole = lax.optimization_barrier((g_in.left, g_gu.whole, g_down.whole))
    while g_out.step < g_out.steps:
        hop_together(g_out, g_in)
    done = (g_out.left, g_out.right, g_in.left, g_in.right)
    w_out = g_out.result()
    gains = w_out[width:].reshape(extra, n_dp, -1).transpose(1, 0, 2).reshape(n_dp, -1).astype(F32)
    w_out = w_out[:width]
    gain_in = gains[:, :part].reshape(1, model)
    gain_ffn = gains[:, part : 2 * part].reshape(1, model)
    gain_group = gains[:, 2 * part : 2 * part + small].reshape(1, HD)
    h1, _ = norm_forward(seq.astype(F32), gain_in)
    w_in = g_in.result()

    gate1 = g_gu.hop(*done)
    up1 = g_up.hop(*done)
    down1 = g_down.hop(*done)
    proj = mm(h1, w_in, NN).astype(BF16)
    y, o, states = rec_forward(proj, seg, gain_group)
    attn_part = after(mm(y, w_out, NN).astype(BF16), *gate1, *up1, *down1)
    g_gu.hop(attn_part)
    g_up.hop(attn_part)
    attn = tensor_scatter_sum(attn_part)
    x = tokens.astype(F32)
    gate3 = g_gu.hop()
    g_down.store()
    x2 = x + g_down.settle(g_gu.settle(after(attn, *gate3, g_up.left, g_up.right)))
    h2_own, r2 = norm_forward(x2, gain_ffn)
    g_up.hop()
    g_gu.hop()
    g_up.hop()
    h2 = g_gu.settle(after(tensor_gather(h2_own), g_gu.left, g_gu.right, g_up.left, g_up.right))
    down2 = g_down.hop(g_up.left, g_up.right)
    g_up.store()
    w_gu = g_gu.result()
    gu = after(mm(h2, w_gu, NN), *down2)
    down3 = g_down.hop(gu)
    gate, up = gu[:, :hidden_width], gu[:, hidden_width:]
    sg = jax.nn.sigmoid(gate)
    swish = gate * sg
    hidden = (swish * up).astype(BF16)
    d_down_part = after(mm(hidden, cot, TN).astype(BF16), *down3)
    down4 = g_down.hop(d_down_part)
    s_down = ring.scatter_sum(d_down_part, 1)
    step1 = s_down.hop()
    w_down = g_down.result()
    dh = mm(after(cot, s_down.left, s_down.right), w_down, NT)
    dgate = (dh * up * sg * (1.0 + gate * (1.0 - sg))).astype(BF16)
    dup = (dh * swish).astype(BF16)
    dgu = jnp.concatenate([dgate, dup], axis=1)
    s_down.hop(during=(dgu,))
    d_gu_part = mm(after(h2, s_down.left, s_down.right), dgu, TN).astype(BF16)
    s_down.hop(during=(d_gu_part,))
    s_gu = ring.scatter_sum(d_gu_part, 0)
    dh2_part = mm(after(dgu, s_gu.left, s_gu.right, s_down.left, s_down.right), w_gu, NT).astype(BF16)
    t1 = s_gu.hop(during=(dh2_part,))
    dh2_part = after(dh2_part, *t1)
    dh2 = tensor_scatter_sum(dh2_part)
    s_gu.hop()
    back2, d_gain_ffn = norm_backward(x2, r2, gain_ffn, after(dh2, s_gu.left, s_gu.right))
    dx2 = cotangent.astype(F32) + back2
    dattn_own = dx2.astype(BF16)
    dattn = tensor_gather(dattn_own)
    ffn_part = mm(after(hidden, dattn_own), w_down, NN).astype(BF16)
    s_gu.hop(during=(ffn_part,))
    dattn = after(dattn, s_gu.left, s_gu.right)
    d_out_part = mm(y, dattn, TN).astype(BF16)
    s_out = ring.scatter_sum(d_out_part, 1)
    ffn = tensor_scatter_sum(after(ffn_part, dattn))
    dy = mm(after(dattn, d_out_part), w_out, NT)
    dproj, d_group = rec_backward(proj, seg, gain_group, o, states, dy)
    t4 = s_gu.hop(during=(dproj,))
    dh1_part = mm(after(dproj, *t4), w_in, NT).astype(BF16)
    dh1 = tensor_scatter_sum(dh1_part)
    step4 = s_down.hop(before=(dproj,), during=(dh1_part,))
    s_out.hop(before=(dproj,), during=(dh1_part,))
    s_in = ring.scatter_sum(mm(after(h1, dh1_part), dproj, TN).astype(BF16), 0)
    s_in.hop(before=step4)
    o2 = s_out.hop(during=(s_in.left, s_in.right))
    r1 = lax.rsqrt(jnp.mean(x * x, axis=-1, keepdims=True) + EPSILON)
    back1, d_gain_in = norm_backward(x, r1, gain_in, after(dh1, s_in.left, s_in.right))
    d_gains = jnp.concatenate(
        [d_gain_in.reshape(n_dp, part), d_gain_ffn.reshape(n_dp, part), d_group.reshape(n_dp, small)], axis=1
    )
    d_gains = lax.psum(d_gains, "tensor")
    s_in.hop(before=o2, during=(d_gains,))
    o3 = s_out.hop(during=(s_in.left, s_in.right))
    d_gains = scatter_sum_small(d_gains, "dp", n_dp)
    s_gu.arrived = after(s_gu.arrived[0], s_in.left, s_in.right), s_gu.arrived[1]
    d_gu = s_gu.finish(2)
    s_in.hop(before=(*o3, d_gains), during=(d_gu,))
    d_gains = d_gains[0]
    d_tokens = after((dx2 + back1).astype(BF16), s_in.left, s_in.right)
    o4 = s_out.hop(during=(s_in.left, s_in.right))
    s_down.arrived = after(s_down.arrived[0], s_in.left, s_in.right), s_down.arrived[1]
    d_down = s_down.result()
    d_out = after(s_out.result(), s_in.left, s_in.right)
    output = (x2 + after(ffn, s_in.left, s_in.right)).astype(BF16)
    s_in.hop(before=o4, during=(d_down, d_tokens))
    d_in = s_in.finish(4)
    return (
        output,
        d_tokens,
        d_in,
        d_out,
        d_gu,
        d_down,
        d_gains[:part],
        d_gains[2 * part :],
        d_gains[part : 2 * part],
    )


def solution(mesh):
    split = P("dp", None, "tensor")
    cross = P("tensor", "dp")
    return jax.shard_map(
        functools.partial(body, mesh.shape["dp"], mesh.shape["tensor"]),
        mesh=mesh,
        in_specs=(SPEC_ROWS, P("dp", None), split, cross, split, cross, P("dp"), P("dp"), P("dp"), SPEC_ROWS),
        out_specs=(SPEC_ROWS, SPEC_ROWS, split, cross, split, cross, P("dp"), P("dp"), P("dp")),
        check_vma=False,
    )
```

```python
import functools
import math
import jax
import jax.numpy as jnp
from jax import lax
from jax.experimental import pallas as pl
from jax.experimental.pallas import tpu as pltpu
from jax.sharding import PartitionSpec as P

HD = 128
CHUNK = 256
GROUP_EPSILON = 0.01
F32 = jnp.float32
BF16 = jnp.bfloat16
NN = (((1,), (0,)), ((), ()))
NT = (((1,), (1,)), ((), ()))
TN = (((0,), (0,)), ((), ()))


def mm(a, b, dims):
    return lax.dot_general(a, b, dims, preferred_element_type=F32)


def halves(x):
    high = x.astype(BF16)
    return high, (x - high.astype(F32)).astype(BF16)


def tri_sum(tri, x):
    high, rest = halves(x)
    return mm(tri, high, NN) + mm(tri, rest, NN)


def decays(a_raw, lower):
    sig = jax.nn.sigmoid(a_raw)
    forget = 0.8 + 0.2 * sig
    key = 1.0 - forget
    cum = tri_sum(lower, jnp.log(forget))
    return sig, forget, key, cum


def masks(seg, doc_col, doc_row, block):
    rows = lax.broadcasted_iota(jnp.int32, (CHUNK, CHUNK), 0)
    cols = lax.broadcasted_iota(jnp.int32, (CHUNK, CHUNK), 1)
    causal = rows >= cols
    same = jnp.logical_and(causal, doc_col == doc_row)
    start = block * CHUNK
    end_doc = seg[start + CHUNK - 1]
    last_doc = jnp.where(block > 0, seg[jnp.maximum(start - 1, 0)], -1)
    cont = (doc_col == last_doc).astype(F32)
    tail = (doc_col == end_doc).astype(F32)
    keep = jnp.where(end_doc == last_doc, 1.0, 0.0).astype(F32)
    return causal, same, cont, tail, keep


def forward_kernel(seg, q_ref, a_ref, v_ref, z_ref, col_ref, row_ref, gain_ref,
                   y_ref, o_ref, s_ref, state):
    block = pl.program_id(0)

    @pl.when(block == 0)
    def _():
        state[...] = jnp.zeros_like(state)

    width = q_ref.shape[1]
    causal, same, cont, tail, keep = masks(seg, col_ref[...], row_ref[...], block)
    lower = jnp.where(causal, 1.0, 0.0).astype(BF16)
    _, _, key, cum = decays(a_ref[...].astype(F32), lower)
    total = cum[CHUNK - 1 : CHUNK, :]
    qd, qd_rest = halves(q_ref[...].astype(F32) * jnp.exp(cum))
    kd, kd_rest = halves(key * jnp.exp(-cum))
    kt, kt_rest = halves(key * jnp.exp(total - cum) * tail)
    fade = jnp.exp(total) * keep
    gain = gain_ref[...]
    s_ref[0] = state[...]
    for head in range(width // HD):
        at = slice(head * HD, (head + 1) * HD)
        v = v_ref[:, at]
        st = state[:, at]
        st_high, st_rest = halves(st)
        qh, ql = qd[:, at], qd_rest[:, at]
        scores = mm(qh, kd[:, at], NT) + (mm(qh, kd_rest[:, at], NT) + mm(ql, kd[:, at], NT))
        scores = jnp.where(same, scores, 0.0).astype(BF16)
        earlier = mm(qh, st_high, NT) + (mm(qh, st_rest, NT) + mm(ql, st_high, NT))
        o = mm(scores, v, NN) + cont * earlier
        state[:, at] = st * fade[:, at] + (mm(v, kt[:, at], TN) + mm(v, kt_rest[:, at], TN))
        o_ref[:, at] = o
        z = z_ref[:, at].astype(F32)
        r = lax.rsqrt(jnp.mean(o * o, axis=-1, keepdims=True) + GROUP_EPSILON)
        y_ref[:, at] = (o * r * gain * (z * jax.nn.sigmoid(z))).astype(BF16)


def backward_kernel(seg, q_ref, a_ref, v_ref, z_ref, col_ref, row_ref, gain_ref, o_ref, s_ref, dy_ref,
                    d_ref, dgain_ref, dstate):
    step = pl.program_id(0)
    block = pl.num_programs(0) - 1 - step

    @pl.when(step == 0)
    def _():
        dstate[...] = jnp.zeros_like(dstate)
        dgain_ref[...] = jnp.zeros_like(dgain_ref)

    width = q_ref.shape[1]
    causal, same, cont, tail, keep = masks(seg, col_ref[...], row_ref[...], block)
    lower = jnp.where(causal, 1.0, 0.0).astype(BF16)
    sig, forget, key, cum = decays(a_ref[...].astype(F32), lower)
    total = cum[CHUNK - 1 : CHUNK, :]
    up = jnp.exp(cum)
    down = jnp.exp(-cum)
    late = jnp.exp(total - cum) * tail
    qd = (q_ref[...].astype(F32) * up).astype(BF16)
    kd = (key * down).astype(BF16)
    kt = (key * late).astype(BF16)
    fade = jnp.exp(total) * keep
    gain = gain_ref[...]
    gain_sum = jnp.zeros((1, HD), F32)
    dcums = []
    dkeys = []
    for head in range(width // HD):
        at = slice(head * HD, (head + 1) * HD)
        v = v_ref[:, at]
        o = o_ref[:, at]
        z = z_ref[:, at].astype(F32)
        dy = dy_ref[:, at]
        r = lax.rsqrt(jnp.mean(o * o, axis=-1, keepdims=True) + GROUP_EPSILON)
        n = o * r
        sz = jax.nn.sigmoid(z)
        dng = dy * (z * sz)
        gain_sum += jnp.sum(dng * n, axis=0, keepdims=True)
        dn = dng * gain
        do = (r * (dn - n * jnp.mean(dn * n, axis=-1, keepdims=True))).astype(BF16)
        d_ref[:, 3 * width + head * HD : 3 * width + (head + 1) * HD] = (
            dy * n * gain * (sz * (1.0 + z * (1.0 - sz)))
        ).astype(BF16)
        qh, kh, th = qd[:, at], kd[:, at], kt[:, at]
        scores = jnp.where(same, mm(qh, kh, NT), 0.0).astype(BF16)
        dscores = jnp.where(same, mm(do, v, NT), 0.0).astype(BF16)
        st = s_ref[0, :, at]
        dst = dstate[:, at]
        dst_low = dst.astype(BF16)
        dv = mm(scores, do, TN) + mm(th, dst_low, NT)
        dqd = mm(dscores, kh, NN) + cont * mm(do, st.astype(BF16), NN)
        dkd = mm(dscores, qh, TN)
        dkt = mm(v, dst_low, NN)
        carried = dkt * th.astype(F32)
        dtotal = jnp.sum(carried, axis=0, keepdims=True) + fade[:, at] * jnp.sum(
            dst * st, axis=0, keepdims=True
        )
        dstate[:, at] = dst * fade[:, at] + mm((do.astype(F32) * cont).astype(BF16), qh, TN)
        d_ref[:, head * HD : (head + 1) * HD] = (dqd * up[:, at]).astype(BF16)
        d_ref[:, 2 * width + head * HD : 2 * width + (head + 1) * HD] = dv.astype(BF16)
        dkeys.append(dkd * down[:, at] + dkt * late[:, at])
        dcum = dqd * qh.astype(F32) - dkd * kh.astype(F32) - carried
        high, rest = halves(dcum)
        dlog = mm(lower, high, TN) + mm(lower, rest, TN) + dtotal
        slope = 0.2 * sig[:, at] * (1.0 - sig[:, at])
        d_ref[:, width + head * HD : width + (head + 1) * HD] = (
            (dlog / forget[:, at] - dkeys[-1]) * slope
        ).astype(BF16)
    dgain_ref[...] += gain_sum


def rec_forward(proj, seg, gain):
    length, width = proj.shape[0], proj.shape[1] // 4
    blocks = length // CHUNK
    part = lambda k: pl.BlockSpec((CHUNK, width), lambda i, s, k=k: (i, k))
    return pl.pallas_call(
        forward_kernel,
        grid_spec=pltpu.PrefetchScalarGridSpec(
            num_scalar_prefetch=1,
            grid=(blocks,),
            in_specs=[part(0), part(1), part(2), part(3),
                      pl.BlockSpec((CHUNK, 1), lambda i, s: (i, 0)),
                      pl.BlockSpec((1, CHUNK), lambda i, s: (0, i)),
                      pl.BlockSpec((1, HD), lambda i, s: (0, 0))],
            out_specs=[pl.BlockSpec((CHUNK, width), lambda i, s: (i, 0)),
                       pl.BlockSpec((CHUNK, width), lambda i, s: (i, 0)),
                       pl.BlockSpec((1, HD, width), lambda i, s: (i, 0, 0))],
            scratch_shapes=[pltpu.VMEM((HD, width), F32)],
        ),
        out_shape=[jax.ShapeDtypeStruct((length, width), BF16),
                   jax.ShapeDtypeStruct((length, width), F32),
                   jax.ShapeDtypeStruct((blocks, HD, width), F32)],
        cost_estimate=pl.CostEstimate(flops=30_000_000_000, bytes_accessed=10_000_000, transcendentals=0),
        name="mixer_forward",
    )(seg, proj, proj, proj, proj, seg.reshape(length, 1), seg.reshape(1, length), gain.reshape(1, HD))


def rec_backward(proj, seg, gain, o, states, dy):
    length, width = proj.shape[0], proj.shape[1] // 4
    blocks = length // CHUNK
    last = blocks - 1
    part = lambda k: pl.BlockSpec((CHUNK, width), lambda i, s, k=k: (last - i, k))
    return pl.pallas_call(
        backward_kernel,
        grid_spec=pltpu.PrefetchScalarGridSpec(
            num_scalar_prefetch=1,
            grid=(blocks,),
            in_specs=[part(0), part(1), part(2), part(3),
                      pl.BlockSpec((CHUNK, 1), lambda i, s: (last - i, 0)),
                      pl.BlockSpec((1, CHUNK), lambda i, s: (0, last - i)),
                      pl.BlockSpec((1, HD), lambda i, s: (0, 0)),
                      part(0),
                      pl.BlockSpec((1, HD, width), lambda i, s: (last - i, 0, 0)),
                      part(0)],
            out_specs=[pl.BlockSpec((CHUNK, 4 * width), lambda i, s: (last - i, 0)),
                       pl.BlockSpec((1, HD), lambda i, s: (0, 0))],
            scratch_shapes=[pltpu.VMEM((HD, width), F32)],
        ),
        out_shape=[jax.ShapeDtypeStruct((length, 4 * width), BF16),
                   jax.ShapeDtypeStruct((1, HD), F32)],
        cost_estimate=pl.CostEstimate(flops=60_000_000_000, bytes_accessed=14_000_000, transcendentals=0),
        name="mixer_backward",
    )(seg, proj, proj, proj, proj, seg.reshape(length, 1), seg.reshape(1, length), gain.reshape(1, HD), o, states, dy)


EPSILON = 1e-06
SPEC_ROWS = P(("dp", "tensor"), None)


def ring_order(count):
    return list(range(0, count, 2)) + list(range(count - 1 - count % 2, 0, -2))


class Ring:
    def __init__(self, axis, count):
        order = ring_order(count)
        self.axis, self.count = axis, count
        self.ahead = [(order[i], order[(i + 1) % count]) for i in range(count)]
        self.behind = [(b, a) for a, b in self.ahead]
        self.me = lax.axis_index(axis)
        self.place = jnp.where(self.me % 2 == 0, self.me // 2, count - (self.me + 1) // 2)

    def owner(self, shift):
        at = (self.place + shift + 2 * self.count) % self.count
        return jnp.where(2 * at < self.count, 2 * at, 2 * (self.count - at) - 1)

    def send_ahead(self, x):
        return lax.ppermute(x, self.axis, self.ahead)

    def send_behind(self, x):
        return lax.ppermute(x, self.axis, self.behind)

    def gather(self, x, dim):
        return Gather(self, x, dim)

    def scatter_sum(self, x, dim):
        return ScatterSum(self, x, dim)


def after(x, *earlier):
    return lax.optimization_barrier((x, *earlier))[0]


def first_kernel(at, block, whole):
    whole[...] = block[...]


def pair_kernel(at, left, right, before, whole):
    @pl.when(pl.program_id(0) == 0)
    def _():
        whole[...] = left[...]

    @pl.when(pl.program_id(0) == 1)
    def _():
        whole[...] = right[...]


SMALL_COST = pl.CostEstimate(flops=0, bytes_accessed=4_000_000, transcendentals=0)


class Gather:
    def __init__(self, ring, x, dim, partner=None):
        self.ring, self.dim, self.half = ring, dim, x.shape[0] // 2
        self.column, self.left, self.right = 0, x, x
        self.step, self.steps, self.pending = 0, ring.count // 2, False
        if partner is not None:
            self.box, self.shape, self.column = partner.box, partner.shape, 1
            return
        shape = list(x.shape)
        shape[dim] *= ring.count
        self.shape = jax.ShapeDtypeStruct(tuple(shape), x.dtype)
        self.aligned = x.shape[1] % 128 == 0
        if not self.aligned:
            at = [0, 0]
            at[dim] = ring.me * x.shape[dim]
            self.box = [lax.dynamic_update_slice(jnp.zeros(shape, x.dtype), x, at)]
            return
        to = (lambda i, at: (at[0], 0)) if self.dim == 0 else (lambda i, at: (0, at[0]))
        self.box = [pl.pallas_call(
            first_kernel,
            grid_spec=pltpu.PrefetchScalarGridSpec(
                num_scalar_prefetch=1, grid=(1,), in_specs=[pl.BlockSpec(x.shape, lambda i, at: (0, 0))],
                out_specs=pl.BlockSpec(x.shape, to)),
            out_shape=self.shape, cost_estimate=SMALL_COST, name="gather_first",
        )(self.ring.me.reshape(1), x)]

    @property
    def whole(self):
        return self.box[0]

    @whole.setter
    def whole(self, value):
        self.box[0] = value

    def hop(self, *earlier):
        ring = self.ring
        left, right = self.left, self.right
        if self.step == self.steps:
            return left, right
        step = self.step + 1
        if step == self.steps:
            left, right = left[: self.half], right[self.half :]
        if step > 1:
            left, right, self.whole, *_ = lax.optimization_barrier((left, right, self.whole, *earlier))
        elif earlier:
            left, right, *_ = lax.optimization_barrier((left, right, *earlier))
        left, right = ring.send_ahead(left), ring.send_behind(right)
        if step > 1:
            self.store()
        self.left, self.right, self.step, self.pending = left, right, step, True
        return left, right

    def halves(self):
        if self.step + 1 == self.steps:
            return self.left[: self.half], self.right[self.half :]
        return self.left, self.right

    def send(self, left, right):
        left, right = self.ring.send_ahead(left), self.ring.send_behind(right)
        self.store()
        self.left, self.right, self.step, self.pending = left, right, self.step + 1, True

    def split(self, x, y):
        self.left = self.right = x
        other = Gather(self.ring, y, self.dim, self)
        other.aligned = self.aligned
        return other

    def settle(self, x):
        x, self.whole = lax.optimization_barrier((x, self.whole))
        return x

    def result(self):
        while self.step < self.steps:
            self.hop()
        self.store()
        return self.whole

    def store(self):
        if not self.pending:
            return
        self.pending = False
        ring = self.ring
        last = self.step == self.steps
        if not self.aligned:
            for block, shift in ((self.left, -self.step), (self.right, self.step)):
                at = [self.half if last and shift > 0 else 0, 0]
                at[self.dim] = at[self.dim] + ring.owner(shift) * self.shape.shape[self.dim] // ring.count
                self.whole = lax.dynamic_update_slice(self.whole, block, at)
            return
        owners = jnp.stack([ring.owner(-self.step), ring.owner(self.step)])
        if self.dim == 0 and last:
            to = lambda i, at: (2 * at[i] + i, self.column)
        elif self.dim == 0:
            to = lambda i, at: (at[i], self.column)
        elif last:
            to = lambda i, at: (i, at[i])
        else:
            to = lambda i, at: (0, at[i])
        block = pl.BlockSpec(self.left.shape, lambda i, at: (0, 0))
        self.whole = pl.pallas_call(
            pair_kernel,
            grid_spec=pltpu.PrefetchScalarGridSpec(
                num_scalar_prefetch=1, grid=(2,),
                in_specs=[block, block, pl.BlockSpec(memory_space=pl.ANY)],
                out_specs=pl.BlockSpec(self.left.shape, to)),
            out_shape=self.shape, input_output_aliases={3: 0}, cost_estimate=SMALL_COST, name="gather_pair",
        )(owners, self.left, self.right, self.whole)


def hop_together(one, two):
    if one.step == one.steps:
        return
    blocks = *one.halves(), *two.halves()
    if one.step:
        *blocks, one.whole, two.whole = lax.optimization_barrier((*blocks, one.whole, two.whole))
    one.send(*blocks[:2])
    two.send(*blocks[2:])


def finish_kernel(parts, at, left, right, own, total):
    both = left[...].astype(F32) + right[...].astype(F32) + own[...].astype(F32)
    width = both.shape[1] // parts
    for k in range(parts):
        total[:, k, :] = both[:, k * width : (k + 1) * width]


class ScatterSum:
    def __init__(self, ring, x, dim):
        self.ring, self.dim, self.x = ring, dim, x
        shape = list(x.shape)
        shape[dim] //= ring.count
        self.size, self.half = shape[dim], shape[0] // 2
        self.shape, self.step, self.steps = shape, 0, ring.count // 2
        self.left = self.part(self.steps)[: self.half]
        self.right = self.part(-self.steps)[self.half :]

    def part(self, shift):
        at = [0, 0]
        at[self.dim] = self.ring.owner(shift) * self.size
        return lax.dynamic_slice(self.x, at, self.shape)

    def hop(self, before=(), during=()):
        ring, left, right = self.ring, self.left, self.right
        if self.step == self.steps:
            return self.arrived
        self.step += 1
        left, right, *_ = lax.optimization_barrier((left, right, *before))
        left, right = ring.send_ahead(left), ring.send_behind(right)
        left, right, *_ = lax.optimization_barrier((left, right, *during))
        self.arrived = left, right
        shift = self.steps - self.step
        if self.step == 1:
            ahead, behind = self.part(shift), self.part(-shift)
            rest, zero = ahead.shape[0] - self.half, jnp.zeros((), left.dtype)
            self.left = lax.pad(left, zero, ((0, rest, 0), (0, 0, 0))) + ahead
            self.right = lax.pad(right, zero, ((self.half, 0, 0), (0, 0, 0))) + behind
        elif shift:
            self.left, self.right = left + self.part(shift), right + self.part(-shift)
        return self.arrived

    def finish(self, parts):
        while self.step < self.steps:
            self.hop()
        left, right = self.arrived
        rows, columns = left.shape
        tile = min(64, rows)
        near = pl.BlockSpec((tile, columns), lambda i, at: (i, 0))
        mine = pl.BlockSpec((tile, columns), lambda i, at: (at[0] * (rows // tile) + i, 0))
        return pl.pallas_call(
            functools.partial(finish_kernel, parts),
            grid_spec=pltpu.PrefetchScalarGridSpec(
                num_scalar_prefetch=1, grid=(rows // tile,), in_specs=[near, near, mine],
                out_specs=pl.BlockSpec((tile, parts, columns // parts), lambda i, at: (i, 0, 0))),
            out_shape=jax.ShapeDtypeStruct((rows, parts, columns // parts), F32),
            cost_estimate=SMALL_COST, name="finish",
        )(self.ring.me.reshape(1), left, right, self.x)

    def result(self):
        while self.step < self.steps:
            self.hop()
        left, right = self.arrived
        return left.astype(F32) + right.astype(F32) + self.part(0).astype(F32)


def gather_small(row, axis, count):
    me = lax.axis_index(axis)
    whole = lax.dynamic_update_slice(jnp.zeros((count, row.shape[1]), row.dtype), row, (me, 0))
    for turn in range(1, count):
        got = lax.ppermute(row, axis, [(i, (i + turn) % count) for i in range(count)])
        whole = lax.dynamic_update_slice(whole, got, ((me - turn + count) % count, 0))
    return whole


def scatter_sum_small(rows, axis, count):
    me = lax.axis_index(axis)
    if count & (count - 1):
        return lax.dynamic_slice_in_dim(lax.psum(rows, axis), me, 1, 0)
    while count > 1:
        count //= 2
        side = me // count % 2
        mine = lax.dynamic_slice_in_dim(rows, side * count, count, 0)
        other = lax.dynamic_slice_in_dim(rows, (1 - side) * count, count, 0)
        whole = lax.axis_size(axis)
        rows = mine + lax.ppermute(other, axis, [(i, i ^ count) for i in range(whole)])
    return rows


def norm_forward(values, gain):
    r = lax.rsqrt(jnp.mean(values * values, axis=-1, keepdims=True) + EPSILON)
    return (values * r * gain).astype(BF16), r


def norm_backward(values, r, gain, grad):
    n = values * r
    scaled = grad * gain
    back = r * (scaled - n * jnp.mean(scaled * n, axis=-1, keepdims=True))
    return back, jnp.sum(grad * n, axis=0)


def tensor_gather(x):
    return lax.all_gather(x, "tensor", axis=0, tiled=True)


def tensor_scatter_sum(x):
    return lax.psum_scatter(x, "tensor", scatter_dimension=0, tiled=True).astype(F32)


def body(n_dp, n_tensor, tokens, segment_ids, mixer_in, mixer_out, gate_up, down,
         norm_gain, group_gain, ffn_gain, cotangent):
    ring = Ring("dp", n_dp)
    seg = segment_ids[0]
    part, small = norm_gain.shape[0], group_gain.shape[0]
    model = part * n_dp
    width = mixer_out.shape[0]
    hidden_width = down.shape[0]

    in_part = mixer_in.reshape(part, 4 * width)
    gu_part = gate_up.reshape(part, 2 * hidden_width)
    extra = 32
    gain_rows = jnp.concatenate([norm_gain, ffn_gain, group_gain])
    gain_rows = jnp.pad(gain_rows, (0, extra * mixer_out.shape[1] - gain_rows.shape[0]))
    out_part = jnp.concatenate([mixer_out, gain_rows.reshape(extra, mixer_out.shape[1])], axis=0)
    seq = tensor_gather(tokens)
    cot = tensor_gather(cotangent)

    g_in, g_out = ring.gather(in_part, 0), ring.gather(out_part, 1)
    hop_together(g_out, g_in)
    g_gu, g_down = ring.gather(gu_part, 0), ring.gather(down, 1)
    g_up = g_gu.split(gu_part[:, :hidden_width], gu_part[:, hidden_width:])
    hop_together(g_out, g_in)
    g_in.left, g_gu.whole, g_down.whole = lax.optimization_barrier((g_in.left, g_gu.whole, g_down.whole))
    while g_out.step < g_out.steps:
        hop_together(g_out, g_in)
    done = (g_out.left, g_out.right, g_in.left, g_in.right)
    w_out = g_out.result()
    gains = w_out[width:].reshape(extra, n_dp, -1).transpose(1, 0, 2).reshape(n_dp, -1).astype(F32)
    w_out = w_out[:width]
    gain_in = gains[:, :part].reshape(1, model)
    gain_ffn = gains[:, part : 2 * part].reshape(1, model)
    gain_group = gains[:, 2 * part : 2 * part + small].reshape(1, HD)
    h1, _ = norm_forward(seq.astype(F32), gain_in)
    w_in = g_in.result()

    gate1 = g_gu.hop(*done)
    up1 = g_up.hop(*done)
    down1 = g_down.hop(*done)
    proj = mm(h1, w_in, NN).astype(BF16)
    y, o, states = rec_forward(proj, seg, gain_group)
    attn_part = after(mm(y, w_out, NN).astype(BF16), *gate1, *up1, *down1)
    g_gu.hop(attn_part)
    g_up.hop(attn_part)
    attn = tensor_scatter_sum(attn_part)
    x = tokens.astype(F32)
    gate3 = g_gu.hop()
    g_down.store()
    x2 = x + g_down.settle(g_gu.settle(after(attn, *gate3, g_up.left, g_up.right)))
    h2_own, r2 = norm_forward(x2, gain_ffn)
    g_up.hop()
    g_gu.hop()
    g_up.hop()
    h2 = g_gu.settle(after(tensor_gather(h2_own), g_gu.left, g_gu.right, g_up.left, g_up.right))
    down2 = g_down.hop(g_up.left, g_up.right)
    g_up.store()
    w_gu = g_gu.result()
    gu = after(mm(h2, w_gu, NN), *down2)
    down3 = g_down.hop(gu)
    gate, up = gu[:, :hidden_width], gu[:, hidden_width:]
    sg = jax.nn.sigmoid(gate)
    swish = gate * sg
    hidden = (swish * up).astype(BF16)
    d_down_part = after(mm(hidden, cot, TN).astype(BF16), *down3)
    down4 = g_down.hop(d_down_part)
    s_down = ring.scatter_sum(d_down_part, 1)
    step1 = s_down.hop()
    w_down = g_down.result()
    dh = mm(after(cot, s_down.left, s_down.right), w_down, NT)
    dgate = (dh * up * sg * (1.0 + gate * (1.0 - sg))).astype(BF16)
    dup = (dh * swish).astype(BF16)
    dgu = jnp.concatenate([dgate, dup], axis=1)
    s_down.hop(during=(dgu,))
    d_gu_part = mm(after(h2, s_down.left, s_down.right), dgu, TN).astype(BF16)
    s_down.hop(during=(d_gu_part,))
    s_gu = ring.scatter_sum(d_gu_part, 0)
    dh2_part = mm(after(dgu, s_gu.left, s_gu.right, s_down.left, s_down.right), w_gu, NT).astype(BF16)
    t1 = s_gu.hop(during=(dh2_part,))
    dh2_part = after(dh2_part, *t1)
    dh2 = tensor_scatter_sum(dh2_part)
    s_gu.hop()
    back2, d_gain_ffn = norm_backward(x2, r2, gain_ffn, after(dh2, s_gu.left, s_gu.right))
    dx2 = cotangent.astype(F32) + back2
    dattn_own = dx2.astype(BF16)
    dattn = tensor_gather(dattn_own)
    ffn_part = mm(after(hidden, dattn_own), w_down, NN).astype(BF16)
    s_gu.hop(during=(ffn_part,))
    dattn = after(dattn, s_gu.left, s_gu.right)
    d_out_part = mm(y, dattn, TN).astype(BF16)
    s_out = ring.scatter_sum(d_out_part, 1)
    ffn = tensor_scatter_sum(after(ffn_part, dattn))
    dy = mm(after(dattn, d_out_part), w_out, NT)
    dproj, d_group = rec_backward(proj, seg, gain_group, o, states, dy)
    t4 = s_gu.hop(during=(dproj,))
    dh1_part = mm(after(dproj, *t4), w_in, NT).astype(BF16)
    dh1 = tensor_scatter_sum(dh1_part)
    step4 = s_down.hop(before=(dproj,), during=(dh1_part,))
    s_out.hop(before=(dproj,), during=(dh1_part,))
    s_in = ring.scatter_sum(mm(after(h1, dh1_part), dproj, TN).astype(BF16), 0)
    s_in.hop(before=step4)
    o2 = s_out.hop(during=(s_in.left, s_in.right))
    r1 = lax.rsqrt(jnp.mean(x * x, axis=-1, keepdims=True) + EPSILON)
    back1, d_gain_in = norm_backward(x, r1, gain_in, after(dh1, s_in.left, s_in.right))
    d_gains = jnp.concatenate(
        [d_gain_in.reshape(n_dp, part), d_gain_ffn.reshape(n_dp, part), d_group.reshape(n_dp, small)], axis=1
    )
    d_gains = lax.psum(d_gains, "tensor")
    s_in.hop(before=o2, during=(d_gains,))
    o3 = s_out.hop(during=(s_in.left, s_in.right))
    d_gains = scatter_sum_small(d_gains, "dp", n_dp)
    s_gu.arrived = after(s_gu.arrived[0], s_in.left, s_in.right), s_gu.arrived[1]
    d_gu = s_gu.finish(2)
    s_in.hop(before=(*o3, d_gains), during=(d_gu,))
    d_gains = d_gains[0]
    d_tokens = after((dx2 + back1).astype(BF16), s_in.left, s_in.right)
    o4 = s_out.hop(during=(s_in.left, s_in.right))
    s_down.arrived = after(s_down.arrived[0], s_in.left, s_in.right), s_down.arrived[1]
    d_down = s_down.result()
    d_out = after(s_out.result(), s_in.left, s_in.right)
    output = (x2 + after(ffn, s_in.left, s_in.right)).astype(BF16)
    s_in.hop(before=o4, during=(d_down, d_tokens))
    d_in = s_in.finish(4)
    return (
        output,
        d_tokens,
        d_in,
        d_out,
        d_gu,
        d_down,
        d_gains[:part],
        d_gains[2 * part :],
        d_gains[part : 2 * part],
    )


def solution(mesh):
    split = P("dp", None, "tensor")
    cross = P("tensor", "dp")
    return jax.shard_map(
        functools.partial(body, mesh.shape["dp"], mesh.shape["tensor"]),
        mesh=mesh,
        in_specs=(SPEC_ROWS, P("dp", None), split, cross, split, cross, P("dp"), P("dp"), P("dp"), SPEC_ROWS),
        out_specs=(SPEC_ROWS, SPEC_ROWS, split, cross, split, cross, P("dp"), P("dp"), P("dp")),
        check_vma=False,
    )
```
